32 devices in a mesh: dp: 4 (over x, core), fsdp: 4 (over z), ctx: 2 (over y).
Axes of the slice: x: 2, y: 2, z: 4, core: 2. Of those that a mesh axis runs over, the one named last changes fastest.
Arguments:
- tokens: bfloat16 [16, 768, 1024], P(('dp', 'fsdp'), 'ctx'), may hold values from -24 to 24
- w_query: bfloat16 [1024, 1024], P(('fsdp', 'ctx'))
- w_key: bfloat16 [1024, 1024], P(('fsdp', 'ctx'))
- w_value: bfloat16 [1024, 1024], P(('fsdp', 'ctx')), may hold values from -0.1875 to 0.1875
- w_output: bfloat16 [1024, 1024], P(('fsdp', 'ctx')), may hold values from -0.1875 to 0.1875
- grad_out: bfloat16 [16, 768, 1024], P(('dp', 'fsdp'), 'ctx'), may hold values from -6 to 6
- doc_lengths: int32 [16, 8], P(('dp', 'fsdp')), may hold values from 1 to 384, 768 in all within a row
- block_ids: int32 [16, 6, 8], replicated, may hold values from 0 to 5, as said below
Outputs:
- layer_out: bfloat16 [16, 768, 1024], P(('dp', 'fsdp'), 'ctx')
- grad_tokens: bfloat16 [16, 768, 1024], P(('dp', 'fsdp'), 'ctx')
- grad_w_query: float32 [1024, 1024], P(('fsdp', 'ctx'))
- grad_w_key: float32 [1024, 1024], P(('fsdp', 'ctx'))
- grad_w_value: float32 [1024, 1024], P(('fsdp', 'ctx'))
- grad_w_output: float32 [1024, 1024], P(('fsdp', 'ctx'))
The draws below stay inside these ranges and needn't reach their ends.
Inputs may be any that keep to these rules, and one draw needn't show every extreme that they name: `doc_lengths`: each row holds 8 lengths that sum to 768; the largest is exactly 384. `block_ids`: for head h and query block j, entries 0, 1, 2 are j - 1, j, j + 1 modulo 6, entry 3 is 0, and the other 4 entries are drawn at random; entries may repeat.
All inputs are finite; a program needn't handle non-finite values.
Results may differ from the reference program's by a relative error of at most 0.039.
Values may be sent and summed in bfloat16 or wider, within the bound.
A program may use at most 128 MiB of HBM per device.

```python
import math
import jax
import jax.numpy as jnp
import numpy as np
from jax import lax

D = 1024
HEADS = 16
HEAD_DIM = 64
BLOCK = 128
NSEL = 8
NDOCS = 8
SEQ = 768
NB = 6
SEQS = 16
TOTAL = 12288


def weight_matrix(key):
    normal = jnp.clip(jax.random.normal(key, (D, D), jnp.float32), -6.0, 6.0)
    return normal * D ** (-0.5)


def draw_w_query(key, part):
    return weight_matrix(jax.random.fold_in(key, 11)).astype(jnp.bfloat16)


def draw_w_key(key, part):
    mixed = weight_matrix(jax.random.fold_in(key, 12))
    return mixed.astype(jnp.bfloat16)


def draw_tokens(key, part):
    shape = (SEQS, SEQ, D)
    mixed = jax.random.normal(jax.random.fold_in(key, 21), shape, jnp.float32)
    return jnp.clip(mixed, -24.0, 24.0).astype(jnp.bfloat16)


def draw_block_ids(key, part):
    positions = lax.broadcasted_iota(jnp.int32, (HEADS, NB, 1), 1)
    window = jnp.concatenate([(positions + NB - 1) % NB, positions, (positions + 1) % NB, jnp.zeros_like(positions)], axis=2)
    drawn_ids = jax.random.randint(jax.random.fold_in(key, 31), (HEADS, NB, NSEL - 4), 0, NB)
    return jnp.concatenate([window, drawn_ids.astype(jnp.int32)], axis=2)


def shard_levels(key, shape, shards, least, high):
    factor_of = 1.0
    for dim, shards_of in shards:
        heights = jax.random.uniform(jax.random.fold_in(jax.random.fold_in(key, 6), dim), (shards_of,), jnp.float32, least / len(shards), high / len(shards))
        factor_of = factor_of * jnp.repeat(jnp.exp(heights), shape[dim] // shards_of).reshape((-1,) + (1,) * (len(shape) - 1 - dim))
    return factor_of


def profile(count, total, bound, lean):
    loads = [(1 << 20) // math.isqrt(standing ** lean) + 1 for standing in range(2, count + 1)]
    rest, holding = total - bound - (count - 1), [1] * (count - 1)
    while rest > 0:
        movable = [i for i in range(count - 1) if holding[i] < bound]
        pool, remaining = sum([loads[i] for i in movable]), rest
        for i in movable:
            more = min(bound - holding[i], max(1, remaining * loads[i] // pool), rest)
            holding[i] = holding[i] + more
            rest = rest - more
    return np.array([bound] + holding)


def ragged_sizes(key, count, total, bound, skew):
    if count == 2:
        one = jax.random.randint(key, (), max(1, total - bound), min(bound, total - 1) + 1)
        return jnp.stack([one, total - one])
    tallies = jnp.asarray(profile(count, total, bound, skew), jnp.int32)
    twos = (count - 1) // 2
    giver, receiver = tallies[1:1 + 2 * twos:2], tallies[2:2 + 2 * twos:2]
    margin = jnp.minimum(giver - 1, bound - receiver)
    moved = jax.random.randint(jax.random.fold_in(key, 1), (twos,), 0, 1 << 20) % (margin + 1)
    tallies = tallies.at[1:1 + 2 * twos:2].set(giver - moved).at[2:2 + 2 * twos:2].set(receiver + moved)
    return tallies[jax.random.permutation(jax.random.fold_in(key, 2), count)]


def scatter_about(own_key, shape, scale, limit, cuts=(), held_as=jnp.bfloat16):
    array = scale * jax.random.normal(own_key, shape, jnp.float32)
    if cuts:
        array = array * shard_levels(own_key, shape, cuts, -0.22, 0.18)
    return jnp.clip(array, -limit, limit).astype(held_as)


def setup_inputs(seed: int = 0) -> dict:
    arg_keys = jax.random.split(jax.random.key(seed), 9)
    tokens = draw_tokens(jax.random.fold_in(arg_keys[8], 71), 0)
    w_query = draw_w_query(jax.random.fold_in(arg_keys[8], 71), 0)
    w_key = draw_w_key(jax.random.fold_in(arg_keys[8], 71), 0)
    w_value = scatter_about(arg_keys[3], (D, D), D ** -0.5, 0.1875, ((0, 8),))
    w_output = scatter_about(arg_keys[4], (D, D), D ** -0.5, 0.1875, ((0, 8),))
    grad_out = scatter_about(arg_keys[5], (SEQS, SEQ, D), 1.0, 6.0, ((0, 16), (1, 2)))
    doc_lengths = jax.vmap(lambda own: ragged_sizes(own, NDOCS, SEQ, SEQ // 2, 2))(jax.random.split(arg_keys[6], SEQS)).reshape((SEQS, NDOCS)).astype(jnp.int32)
    block_ids = draw_block_ids(jax.random.fold_in(arg_keys[8], 71), 0)
    return dict(tokens=tokens, w_query=w_query, w_key=w_key, w_value=w_value, w_output=w_output, grad_out=grad_out, doc_lengths=doc_lengths, block_ids=block_ids)


def segment_ids(lengths, count):
    doc_ends = jnp.cumsum(lengths)
    places = jnp.arange(count, dtype=jnp.int32)
    return jnp.sum((places[None, :] >= doc_ends[:, None]).astype(jnp.int32), axis=0)


def rounded(matrix):
    return lax.optimization_barrier(matrix.astype(jnp.bfloat16)).astype(jnp.float32)


def head_pass(head_item, segments):
    queries, keys_in, values_in, grads_in, blocks = head_item
    scale_factor = HEAD_DIM ** -0.5
    flat_ids = blocks.reshape(-1)
    query_blocks = queries.reshape(NB, BLOCK, HEAD_DIM).astype(jnp.float32)
    key_blocks = keys_in.reshape(NB, BLOCK, HEAD_DIM)[flat_ids].reshape(NB, NSEL * BLOCK, HEAD_DIM).astype(jnp.float32)
    value_blocks = values_in.reshape(NB, BLOCK, HEAD_DIM)[flat_ids].reshape(NB, NSEL * BLOCK, HEAD_DIM).astype(jnp.float32)
    grad_blocks = grads_in.reshape(NB, BLOCK, HEAD_DIM).astype(jnp.float32)
    query_segs = segments.reshape(NB, BLOCK)
    key_segs = segments.reshape(NB, BLOCK)[flat_ids].reshape(NB, NSEL * BLOCK)
    live_mask = query_segs[:, :, None] == key_segs[:, None, :]
    scores = jnp.einsum("nqd,nkd->nqk", query_blocks, key_blocks) * scale_factor
    scores = jnp.where(live_mask, scores, -1e30)
    top_score = jnp.max(scores, axis=2, keepdims=True)
    weights = jnp.where(live_mask, jnp.exp(scores - top_score), 0.0)
    soft_probs = weights / jnp.sum(weights, axis=2, keepdims=True)
    probs_bf = rounded(soft_probs)
    attended = jnp.einsum("nqk,nkd->nqd", probs_bf, value_blocks).astype(jnp.bfloat16)
    row_delta = jnp.sum(grad_blocks * attended.astype(jnp.float32), axis=2, keepdims=True)
    d_probs = jnp.einsum("nqd,nkd->nqk", grad_blocks, value_blocks)
    d_scores = rounded(soft_probs * (d_probs - row_delta) * scale_factor)
    d_queries = jnp.einsum("nqk,nkd->nqd", d_scores, key_blocks).astype(jnp.bfloat16)
    key_terms = jnp.einsum("nqk,nqd->nkd", d_scores, query_blocks).reshape(NB * NSEL, BLOCK * HEAD_DIM)
    value_terms = jnp.einsum("nqk,nqd->nkd", probs_bf, grad_blocks).reshape(NB * NSEL, BLOCK * HEAD_DIM)
    d_keys = jax.ops.segment_sum(key_terms, flat_ids, num_segments=NB).astype(jnp.bfloat16)
    d_values = jax.ops.segment_sum(value_terms, flat_ids, num_segments=NB).astype(jnp.bfloat16)
    return (attended.reshape(SEQ, HEAD_DIM), d_queries.reshape(SEQ, HEAD_DIM),
            d_keys.reshape(SEQ, HEAD_DIM), d_values.reshape(SEQ, HEAD_DIM))


def split_heads(matrix):
    return matrix.reshape(SEQ, HEADS, HEAD_DIM).transpose(1, 0, 2)


def join_heads(matrix):
    return matrix.transpose(1, 0, 2).reshape(SEQ, D)


def reference(tokens, w_query, w_key, w_value, w_output, grad_out, doc_lengths, block_ids):
    def one_sequence(totals, inputs):
        tok_rows, cotangent, lengths = inputs
        segments = segment_ids(lengths, SEQ)
        queries = jnp.dot(tok_rows, w_query, preferred_element_type=jnp.float32).astype(jnp.bfloat16)
        keys_all = jnp.dot(tok_rows, w_key, preferred_element_type=jnp.float32).astype(jnp.bfloat16)
        values_all = jnp.dot(tok_rows, w_value, preferred_element_type=jnp.float32).astype(jnp.bfloat16)
        d_attended = jnp.dot(cotangent, w_output.T, preferred_element_type=jnp.float32).astype(jnp.bfloat16)

        def per_head(head_item):
            return head_pass(head_item, segments)

        results = lax.map(per_head, (split_heads(queries), split_heads(keys_all), split_heads(values_all),
                                     split_heads(d_attended), block_ids))
        attended = join_heads(results[0])
        d_queries = join_heads(results[1])
        d_keys = join_heads(results[2])
        d_values = join_heads(results[3])
        layer_out = (tok_rows.astype(jnp.float32)
                     + jnp.dot(attended, w_output, preferred_element_type=jnp.float32)).astype(jnp.bfloat16)
        grad_tokens = (cotangent.astype(jnp.float32)
                       + jnp.dot(d_queries, w_query.T, preferred_element_type=jnp.float32)
                       + jnp.dot(d_keys, w_key.T, preferred_element_type=jnp.float32)
                       + jnp.dot(d_values, w_value.T, preferred_element_type=jnp.float32)).astype(jnp.bfloat16)
        additions = (jnp.dot(tok_rows.T, d_queries, preferred_element_type=jnp.float32),
                     jnp.dot(tok_rows.T, d_keys, preferred_element_type=jnp.float32),
                     jnp.dot(tok_rows.T, d_values, preferred_element_type=jnp.float32),
                     jnp.dot(attended.T, cotangent, preferred_element_type=jnp.float32))
        totals = (totals[0] + additions[0], totals[1] + additions[1],
                  totals[2] + additions[2], totals[3] + additions[3])
        return totals, (layer_out, grad_tokens)

    zero_grad = jnp.zeros((D, D), jnp.float32)
    totals, outputs = lax.scan(one_sequence, (zero_grad, zero_grad, zero_grad, zero_grad),
                               (tokens, grad_out, doc_lengths))
    grad_scale = TOTAL ** -0.5
    return (outputs[0], outputs[1], totals[0] * grad_scale, totals[1] * grad_scale,
            totals[2] * grad_scale, totals[3] * grad_scale)
```

```python
import math

import jax
import jax.numpy as jnp
from jax import lax
from jax.experimental import pallas as pl
from jax.experimental.pallas import tpu as pltpu
from jax.sharding import PartitionSpec as P

HEADS = 16
HEAD_DIM = 64
BLOCK = 128


def contract_last(left_rows, right_rows):
    return lax.dot_general(
        left_rows, right_rows, (((1,), (1,)), ((), ())), preferred_element_type=jnp.float32
    )


def contract_first(left_rows, right_rows):
    return lax.dot_general(
        left_rows, right_rows, (((0,), (0,)), ((), ())), preferred_element_type=jnp.float32
    )


def segment_ids(lengths, count):
    doc_ends = jnp.cumsum(lengths)
    places = lax.broadcasted_iota(jnp.int32, (lengths.shape[0], count), 1)
    return jnp.sum((places >= doc_ends[:, None]).astype(jnp.int32), axis=0)


def head_pass(queries, keys_in, values_in, grads_in, blocks, segments):
    seq_len, head_dim = queries.shape
    block_count = seq_len // BLOCK
    select = blocks.shape[1]
    group_size = math.gcd(block_count, max(1, 512 // BLOCK))
    scale_factor = head_dim ** (-0.5)
    query_blocks = queries.reshape(block_count, BLOCK, head_dim)
    key_blocks = keys_in.reshape(block_count, BLOCK, head_dim)
    value_blocks = values_in.reshape(block_count, BLOCK, head_dim)
    grad_blocks = grads_in.reshape(block_count, BLOCK, head_dim)
    seg_blocks = segments.reshape(block_count, BLOCK)
    owner_rows = lax.broadcasted_iota(jnp.int32, (block_count, group_size * select), 0)

    def one_group(carried, group_index):
        key_acc, value_acc = carried
        first_block = group_index * group_size
        chosen = lax.dynamic_slice_in_dim(blocks, first_block, group_size, 0).reshape(-1)
        query_part = lax.dynamic_slice_in_dim(query_blocks, first_block, group_size, 0)
        grad_part = lax.dynamic_slice_in_dim(grad_blocks, first_block, group_size, 0)
        query_segs = lax.dynamic_slice_in_dim(seg_blocks, first_block, group_size, 0)
        key_part = key_blocks[chosen].reshape(group_size, select * BLOCK, head_dim)
        value_part = value_blocks[chosen].reshape(group_size, select * BLOCK, head_dim)
        key_segs = seg_blocks[chosen].reshape(group_size, select * BLOCK)
        live_mask = query_segs[:, :, None] == key_segs[:, None, :]
        scores = (
            jnp.einsum("nqd,nkd->nqk", query_part, key_part, preferred_element_type=jnp.float32)
            * scale_factor
        )
        scores = jnp.where(live_mask, scores, -1e30)
        top_score = jnp.max(scores, axis=2, keepdims=True)
        weights = jnp.where(live_mask, jnp.exp(scores - top_score), 0.0)
        soft_probs = weights / jnp.sum(weights, axis=2, keepdims=True)
        probs_bf = soft_probs.astype(jnp.bfloat16)
        attended = jnp.einsum(
            "nqk,nkd->nqd", probs_bf, value_part, preferred_element_type=jnp.float32
        ).astype(jnp.bfloat16)
        row_delta = jnp.sum(
            grad_part.astype(jnp.float32) * attended.astype(jnp.float32), axis=2, keepdims=True
        )
        d_probs = jnp.einsum(
            "nqd,nkd->nqk", grad_part, value_part, preferred_element_type=jnp.float32
        )
        d_scores = (soft_probs * (d_probs - row_delta) * scale_factor).astype(jnp.bfloat16)
        d_query = jnp.einsum(
            "nqk,nkd->nqd", d_scores, key_part, preferred_element_type=jnp.float32
        ).astype(jnp.bfloat16)
        key_terms = jnp.einsum(
            "nqk,nqd->nkd", d_scores, query_part, preferred_element_type=jnp.float32
        ).reshape(group_size * select, BLOCK * head_dim)
        value_terms = jnp.einsum(
            "nqk,nqd->nkd", probs_bf, grad_part, preferred_element_type=jnp.float32
        ).reshape(group_size * select, BLOCK * head_dim)
        owner_map = (owner_rows == chosen[None, :]).astype(jnp.float32)
        key_acc = key_acc + jnp.dot(
            owner_map,
            key_terms,
            precision=lax.Precision.HIGHEST,
            preferred_element_type=jnp.float32,
        )
        value_acc = value_acc + jnp.dot(
            owner_map,
            value_terms,
            precision=lax.Precision.HIGHEST,
            preferred_element_type=jnp.float32,
        )
        return ((key_acc, value_acc), (attended, d_query))

    blank_acc = jnp.zeros((block_count, BLOCK * head_dim), jnp.float32)
    sums, stacked = lax.scan(
        one_group, (blank_acc, blank_acc), jnp.arange(block_count // group_size, dtype=jnp.int32)
    )
    return (
        stacked[0].reshape(seq_len, head_dim),
        stacked[1].reshape(seq_len, head_dim),
        sums[0].reshape(seq_len, head_dim).astype(jnp.bfloat16),
        sums[1].reshape(seq_len, head_dim).astype(jnp.bfloat16),
    )


def general_device(tokens, w_query, w_key, w_value, w_output, grad_out, doc_lengths, block_ids):
    tok_rows = tokens[0]
    cotangent = grad_out[0]
    tok_dev, width = tok_rows.shape
    ctx_size = lax.axis_size("ctx")
    local_heads = HEADS // ctx_size
    head_band = local_heads * HEAD_DIM
    group_rows = (
        lax.all_gather(w_query, "ctx", axis=0, tiled=True),
        lax.all_gather(w_key, "ctx", axis=0, tiled=True),
        lax.all_gather(w_value, "ctx", axis=0, tiled=True),
        lax.all_gather(w_output, "ctx", axis=0, tiled=True),
    )
    pieces = (
        lax.all_gather(group_rows[0], "fsdp", axis=0, tiled=True),
        lax.all_gather(group_rows[1], "fsdp", axis=0, tiled=True),
        lax.all_gather(group_rows[2], "fsdp", axis=0, tiled=True),
        lax.all_gather(group_rows[3], "fsdp", axis=0, tiled=True),
    )
    tok_part = tok_rows
    query_acc = jnp.dot(tok_part, pieces[0], preferred_element_type=jnp.float32)
    key_acc = jnp.dot(tok_part, pieces[1], preferred_element_type=jnp.float32)
    value_acc = jnp.dot(tok_part, pieces[2], preferred_element_type=jnp.float32)
    grad_acc = contract_last(cotangent, pieces[3])
    queries = query_acc.astype(jnp.bfloat16)
    keys_all = key_acc.astype(jnp.bfloat16)
    values_all = value_acc.astype(jnp.bfloat16)
    d_attended = grad_acc.astype(jnp.bfloat16)

    def to_band(matrix):
        return matrix.reshape(tok_dev, ctx_size, head_band)

    received = (
        lax.all_to_all(to_band(queries), "ctx", split_axis=1, concat_axis=0, tiled=True),
        lax.all_to_all(to_band(keys_all), "ctx", split_axis=1, concat_axis=0, tiled=True),
        lax.all_to_all(to_band(values_all), "ctx", split_axis=1, concat_axis=0, tiled=True),
        lax.all_to_all(to_band(d_attended), "ctx", split_axis=1, concat_axis=0, tiled=True),
    )
    query_heads = received[0].reshape(-1, head_band)
    key_heads = received[1].reshape(-1, head_band)
    value_heads = received[2].reshape(-1, head_band)
    grad_heads = received[3].reshape(-1, head_band)
    seq_len = query_heads.shape[0]
    segments = segment_ids(doc_lengths[0], seq_len)
    head_base = lax.axis_index("ctx") * local_heads

    def per_head(head_index, buffers):
        column = head_index * HEAD_DIM

        def columns(matrix):
            return lax.dynamic_slice_in_dim(matrix, column, HEAD_DIM, 1)

        blocks = lax.dynamic_slice_in_dim(block_ids, head_base + head_index, 1, 0)[0]
        results = head_pass(
            columns(query_heads),
            columns(key_heads),
            columns(value_heads),
            columns(grad_heads),
            blocks,
            segments,
        )
        return (
            lax.dynamic_update_slice_in_dim(buffers[0], results[0], column, 1),
            lax.dynamic_update_slice_in_dim(buffers[1], results[1], column, 1),
            lax.dynamic_update_slice_in_dim(buffers[2], results[2], column, 1),
            lax.dynamic_update_slice_in_dim(buffers[3], results[3], column, 1),
        )

    blank_band = jnp.zeros((seq_len, head_band), jnp.bfloat16)
    buffers = lax.fori_loop(
        0, local_heads, per_head, (blank_band, blank_band, blank_band, blank_band)
    )

    def to_rows(matrix):
        return matrix.reshape(seq_len, 1, head_band)

    returned = (
        lax.all_to_all(to_rows(buffers[0]), "ctx", split_axis=0, concat_axis=1, tiled=True),
        lax.all_to_all(to_rows(buffers[1]), "ctx", split_axis=0, concat_axis=1, tiled=True),
        lax.all_to_all(to_rows(buffers[2]), "ctx", split_axis=0, concat_axis=1, tiled=True),
        lax.all_to_all(to_rows(buffers[3]), "ctx", split_axis=0, concat_axis=1, tiled=True),
    )
    attended = returned[0].reshape(tok_dev, width)
    d_query = returned[1].reshape(tok_dev, width)
    d_key = returned[2].reshape(tok_dev, width)
    d_value = returned[3].reshape(tok_dev, width)
    pieces = (
        lax.all_gather(group_rows[0], "fsdp", axis=0, tiled=True),
        lax.all_gather(group_rows[1], "fsdp", axis=0, tiled=True),
        lax.all_gather(group_rows[2], "fsdp", axis=0, tiled=True),
        lax.all_gather(group_rows[3], "fsdp", axis=0, tiled=True),
    )
    out_acc = tok_rows.astype(jnp.float32)
    att_part = attended
    out_acc = out_acc + jnp.dot(att_part, pieces[3], preferred_element_type=jnp.float32)
    update = (
        contract_last(d_query, pieces[0])
        + contract_last(d_key, pieces[1])
        + contract_last(d_value, pieces[2])
    )
    grad_acc = update
    layer_out = out_acc.astype(jnp.bfloat16)
    grad_tokens = (cotangent.astype(jnp.float32) + grad_acc).astype(jnp.bfloat16)
    total_tokens = tok_dev * lax.axis_size("dp") * lax.axis_size("fsdp") * ctx_size
    grad_scale = total_tokens ** (-0.5)
    tok_part = tok_rows
    att_part = attended
    summed = lax.psum_scatter(
        jnp.concatenate(
            [
                contract_first(tok_part, d_query),
                contract_first(tok_part, d_key),
                contract_first(tok_part, d_value),
                contract_first(att_part, cotangent),
            ],
            axis=1,
        )
        * grad_scale,
        ("fsdp", "ctx"),
        scatter_dimension=0,
        tiled=True,
    )
    summed = lax.psum(summed, "dp")
    return (
        layer_out[None],
        grad_tokens[None],
        summed[:, 0:width],
        summed[:, width : 2 * width],
        summed[:, 2 * width : 3 * width],
        summed[:, 3 * width : 4 * width],
    )


def attention_kernel(
    logs_ref, seg_row_ref, seg_col_ref, q_ref, k_ref, v_ref, g_ref,
    att_ref, dq_ref, dk_ref, dv_ref, dk_acc, dv_acc,
):
    seq_len, lanes = q_ref.shape
    heads_here = lanes // HEAD_DIM
    block_count = seq_len // BLOCK
    tile = BLOCK * (2 if block_count % 2 == 0 else 1)
    scale_factor = HEAD_DIM ** (-0.5)
    lane_ids = lax.broadcasted_iota(jnp.int32, (1, lanes), 1) // HEAD_DIM
    keys = k_ref[...]
    values = v_ref[...]
    dk_acc[...] = jnp.zeros_like(dk_acc)
    dv_acc[...] = jnp.zeros_like(dv_acc)
    seg_keys = seg_col_ref[...]
    zero = jnp.zeros((), jnp.bfloat16)

    for part in range(seq_len // tile):
        rows = pl.ds(part * tile, tile)
        query_part = q_ref[rows, :] * jnp.asarray(scale_factor, jnp.bfloat16)
        grad_part = g_ref[rows, :]
        live = seg_keys == seg_row_ref[:, rows]
        att_sum = jnp.zeros((tile, lanes), jnp.float32)
        dq_sum = jnp.zeros((tile, lanes), jnp.float32)
        for head in range(heads_here):
            mine = lane_ids == head
            q_head = jnp.where(mine, query_part, zero)
            g_head = jnp.where(mine, grad_part, zero)
            scores = contract_last(keys, q_head)
            bias = jnp.broadcast_to(
                logs_ref[head, :, rows][:, None, :], (block_count, BLOCK, tile)
            ).reshape(seq_len, tile)
            scores = jnp.where(live, scores + bias, -1e30)
            top_score = jnp.max(scores, axis=0, keepdims=True)
            weights = jnp.exp(scores - top_score)
            inverse = 1.0 / jnp.sum(weights, axis=0, keepdims=True)
            probs = weights * inverse
            d_probs = contract_last(values, g_head)
            row_delta = jnp.sum(probs * d_probs, axis=0, keepdims=True)
            probs_bf = probs.astype(jnp.bfloat16)
            d_scores = (probs * (d_probs - row_delta)).astype(jnp.bfloat16)
            att_sum = jnp.where(mine, contract_first(probs_bf, values), att_sum)
            dq_sum = jnp.where(mine, contract_first(d_scores, keys), dq_sum)
            dv_acc[...] += jnp.dot(probs_bf, g_head, preferred_element_type=jnp.float32)
            dk_acc[...] += jnp.dot(d_scores, q_head, preferred_element_type=jnp.float32)
        att_ref[rows, :] = att_sum.astype(jnp.bfloat16)
        dq_ref[rows, :] = (dq_sum * scale_factor).astype(jnp.bfloat16)
    dk_ref[...] = dk_acc[...].astype(jnp.bfloat16)
    dv_ref[...] = dv_acc[...].astype(jnp.bfloat16)


def attention(queries, keys, values, grads, logs, segments, stripe):
    seq_len, band = queries.shape
    heads_here = stripe // HEAD_DIM
    block_count = logs.shape[1]
    whole = pl.BlockSpec((seq_len, stripe), lambda i: (0, i))
    return pl.pallas_call(
        attention_kernel,
        grid=(band // stripe,),
        out_shape=[jax.ShapeDtypeStruct((seq_len, band), jnp.bfloat16)] * 4,
        in_specs=[
            pl.BlockSpec((heads_here, block_count, seq_len), lambda i: (i, 0, 0)),
            pl.BlockSpec((1, seq_len), lambda i: (0, 0)),
            pl.BlockSpec((seq_len, 1), lambda i: (0, 0)),
            whole, whole, whole, whole,
        ],
        out_specs=[whole] * 4,
        scratch_shapes=[pltpu.VMEM((seq_len, stripe), jnp.float32)] * 2,
        compiler_params=pltpu.CompilerParams(vmem_limit_bytes=48 * 1024 * 1024),
        name="attention",
    )(logs, segments[None, :], segments[:, None], queries, keys, values, grads)


def block_logs(blocks, seq_len):
    block_count = blocks.shape[1]
    ids = jnp.arange(block_count, dtype=jnp.int32)
    counts = jnp.sum((blocks[:, None, :, :] == ids[None, :, None, None]).astype(jnp.float32), 3)
    logs = jnp.where(counts > 0, jnp.log(jnp.maximum(counts, 1.0)), -1e30)
    return jnp.repeat(logs, seq_len // block_count, axis=2)


def striped_device(tokens, w_query, w_key, w_value, w_output, grad_out, doc_lengths, block_ids):
    tok_rows = tokens[0]
    cotangent = grad_out[0]
    tok_dev, width = tok_rows.shape
    rows = w_query.shape[0]
    dp_size, fsdp_size = lax.axis_size("dp"), lax.axis_size("fsdp")
    ctx_size = 2
    me = lax.axis_index("ctx")
    swap = [(0, 1), (1, 0)]
    band = fsdp_size * rows
    seq_len = tok_dev * ctx_size
    share = rows // dp_size

    def other(matrix):
        return lax.ppermute(matrix, "ctx", swap)

    def ordered(own, peer):
        first = me == 0
        return jnp.stack([jnp.where(first, own, peer), jnp.where(first, peer, own)])

    tok_peer = other(tok_rows)
    cot_peer = other(cotangent)

    start = lax.axis_index("dp") * share

    def my_share(matrix):
        return lax.dynamic_slice_in_dim(matrix, start, share, 0)

    qkv = jnp.stack([my_share(w_query), my_share(w_key), my_share(w_value)], axis=1)
    qkv = qkv.reshape(share, 3, fsdp_size, ctx_size, rows)
    kept = lax.dynamic_index_in_dim(qkv, me, 3, False).reshape(share, 3 * band)
    sent = lax.dynamic_index_in_dim(qkv, 1 - me, 3, False).reshape(share, 3 * band)
    qkv = ordered(kept, other(sent))
    out_share = my_share(w_output).reshape(share, ctx_size, width // 2).transpose(1, 0, 2)
    packed = jnp.concatenate([qkv, out_share], axis=2)
    gathered = lax.all_gather(packed, ("fsdp", "dp"), axis=0, tiled=False)
    gathered = gathered.reshape(fsdp_size, dp_size, ctx_size, share, 3 * band + width // 2)
    w_qkv = gathered[..., : 3 * band].transpose(0, 2, 1, 3, 4).reshape(width, 3 * band)
    w_out = gathered[..., 3 * band :].transpose(0, 1, 3, 2, 4).reshape(band, width)

    tok_all = ordered(tok_rows, tok_peer).reshape(seq_len, width)
    cot_all = ordered(cotangent, cot_peer).reshape(seq_len, width)
    queries = jnp.dot(
        tok_all, w_qkv[:, :band], preferred_element_type=jnp.float32
    ).astype(jnp.bfloat16)
    keys = jnp.dot(
        tok_all, w_qkv[:, band : 2 * band], preferred_element_type=jnp.float32
    ).astype(jnp.bfloat16)
    values = jnp.dot(
        tok_all, w_qkv[:, 2 * band :], preferred_element_type=jnp.float32
    ).astype(jnp.bfloat16)
    d_attended = contract_last(cot_all, w_out).astype(jnp.bfloat16)

    segments = segment_ids(doc_lengths[0], seq_len)
    stripe_heads = rows // HEAD_DIM
    my_blocks = lax.dynamic_index_in_dim(
        block_ids.reshape((fsdp_size, ctx_size, stripe_heads) + block_ids.shape[1:]), me, 1, False
    ).reshape((fsdp_size * stripe_heads,) + block_ids.shape[1:])
    logs = block_logs(my_blocks, seq_len)
    attended, d_query, d_key, d_value = attention(
        queries, keys, values, d_attended, logs, segments, rows
    )
    d_qkv = jnp.concatenate([d_query, d_key, d_value], axis=1)

    total_tokens = tok_dev * dp_size * fsdp_size * ctx_size
    grad_scale = total_tokens ** (-0.5)
    g_qkv = (contract_first(tok_all, d_qkv) * grad_scale).astype(jnp.bfloat16)
    g_out = (contract_first(attended, cot_all) * grad_scale).astype(jnp.bfloat16)
    g_qkv = g_qkv.reshape(fsdp_size, ctx_size, dp_size, share, 3 * band).transpose(2, 0, 1, 3, 4)
    g_out = g_out.reshape(fsdp_size, dp_size, share, ctx_size, width // 2).transpose(1, 0, 3, 2, 4)
    partial = jnp.concatenate([g_qkv, g_out], axis=4)
    summed = lax.psum_scatter(partial, "dp", scatter_dimension=0, tiled=False)
    summed = lax.psum_scatter(summed, "fsdp", scatter_dimension=0, tiled=False)
    s_qkv = summed[..., : 3 * band]
    kept = lax.dynamic_index_in_dim(s_qkv, me, 0, False)
    sent = lax.dynamic_index_in_dim(s_qkv, 1 - me, 0, False)
    final = jnp.concatenate([ordered(kept, other(sent)), summed[..., 3 * band :]], axis=2)
    final = lax.all_gather(final, "dp", axis=0, tiled=False)
    f_qkv = final[..., : 3 * band].reshape(dp_size, ctx_size, share, 3, fsdp_size, rows)
    f_qkv = f_qkv.transpose(3, 0, 2, 4, 1, 5).reshape(3, rows, width).astype(jnp.float32)
    f_out = final[..., 3 * band :].transpose(0, 2, 1, 3).reshape(rows, width).astype(jnp.float32)

    out_part = jnp.dot(attended, w_out, preferred_element_type=jnp.float32)
    tok_part = contract_last(d_qkv, w_qkv)
    out_part = out_part.reshape(ctx_size, tok_dev, width)
    tok_part = tok_part.reshape(ctx_size, tok_dev, width)

    def pick(matrix, index):
        return lax.dynamic_index_in_dim(matrix, index, 0, False)

    out_sent = other(pick(out_part, 1 - me).astype(jnp.bfloat16))
    tok_sent = other(pick(tok_part, 1 - me).astype(jnp.bfloat16))
    layer_out = tok_rows.astype(jnp.float32) + pick(out_part, me) + out_sent.astype(jnp.float32)
    grad_tokens = cotangent.astype(jnp.float32) + pick(tok_part, me) + tok_sent.astype(jnp.float32)
    return (
        layer_out.astype(jnp.bfloat16)[None],
        grad_tokens.astype(jnp.bfloat16)[None],
        f_qkv[0],
        f_qkv[1],
        f_qkv[2],
        f_out,
    )


def per_device(tokens, w_query, w_key, w_value, w_output, grad_out, doc_lengths, block_ids):
    rows = w_query.shape[0]
    dp_size = lax.axis_size("dp")
    striped = (
        lax.axis_size("ctx") == 2
        and rows % 128 == 0
        and rows % HEAD_DIM == 0
        and rows % (dp_size * 16) == 0
    )
    body = striped_device if striped else general_device
    return body(tokens, w_query, w_key, w_value, w_output, grad_out, doc_lengths, block_ids)


def solution(mesh):
    in_specs = (
        P(("dp", "fsdp"), "ctx", None),
        P(("fsdp", "ctx"), None),
        P(("fsdp", "ctx"), None),
        P(("fsdp", "ctx"), None),
        P(("fsdp", "ctx"), None),
        P(("dp", "fsdp"), "ctx", None),
        P(("dp", "fsdp"), None),
        P(),
    )
    out_specs = (
        P(("dp", "fsdp"), "ctx", None),
        P(("dp", "fsdp"), "ctx", None),
        P(("fsdp", "ctx"), None),
        P(("fsdp", "ctx"), None),
        P(("fsdp", "ctx"), None),
        P(("fsdp", "ctx"), None),
    )
    return jax.shard_map(
        per_device, mesh=mesh, in_specs=in_specs, out_specs=out_specs, check_vma=False
    )
```

```python
import math

import jax
import jax.numpy as jnp
from jax import lax
from jax.experimental import pallas as pl
from jax.experimental.pallas import tpu as pltpu
from jax.sharding import PartitionSpec as P

HEADS = 16
HEAD_DIM = 64
BLOCK = 128


def contract_last(left_rows, right_rows):
    return lax.dot_general(
        left_rows, right_rows, (((1,), (1,)), ((), ())), preferred_element_type=jnp.float32
    )


def contract_first(left_rows, right_rows):
    return lax.dot_general(
        left_rows, right_rows, (((0,), (0,)), ((), ())), preferred_element_type=jnp.float32
    )


def segment_ids(lengths, count):
    doc_ends = jnp.cumsum(lengths)
    places = lax.broadcasted_iota(jnp.int32, (lengths.shape[0], count), 1)
    return jnp.sum((places >= doc_ends[:, None]).astype(jnp.int32), axis=0)


def head_pass(queries, keys_in, values_in, grads_in, blocks, segments):
    seq_len, head_dim = queries.shape
    block_count = seq_len // BLOCK
    select = blocks.shape[1]
    group_size = math.gcd(block_count, max(1, 512 // BLOCK))
    scale_factor = head_dim ** (-0.5)
    query_blocks = queries.reshape(block_count, BLOCK, head_dim)
    key_blocks = keys_in.reshape(block_count, BLOCK, head_dim)
    value_blocks = values_in.reshape(block_count, BLOCK, head_dim)
    grad_blocks = grads_in.reshape(block_count, BLOCK, head_dim)
    seg_blocks = segments.reshape(block_count, BLOCK)
    owner_rows = lax.broadcasted_iota(jnp.int32, (block_count, group_size * select), 0)

    def one_group(carried, group_index):
        key_acc, value_acc = carried
        first_block = group_index * group_size
        chosen = lax.dynamic_slice_in_dim(blocks, first_block, group_size, 0).reshape(-1)
        query_part = lax.dynamic_slice_in_dim(query_blocks, first_block, group_size, 0)
        grad_part = lax.dynamic_slice_in_dim(grad_blocks, first_block, group_size, 0)
        query_segs = lax.dynamic_slice_in_dim(seg_blocks, first_block, group_size, 0)
        key_part = key_blocks[chosen].reshape(group_size, select * BLOCK, head_dim)
        value_part = value_blocks[chosen].reshape(group_size, select * BLOCK, head_dim)
        key_segs = seg_blocks[chosen].reshape(group_size, select * BLOCK)
        live_mask = query_segs[:, :, None] == key_segs[:, None, :]
        scores = (
            jnp.einsum("nqd,nkd->nqk", query_part, key_part, preferred_element_type=jnp.float32)
            * scale_factor
        )
        scores = jnp.where(live_mask, scores, -1e30)
        top_score = jnp.max(scores, axis=2, keepdims=True)
        weights = jnp.where(live_mask, jnp.exp(scores - top_score), 0.0)
        soft_probs = weights / jnp.sum(weights, axis=2, keepdims=True)
        probs_bf = soft_probs.astype(jnp.bfloat16)
        attended = jnp.einsum(
            "nqk,nkd->nqd", probs_bf, value_part, preferred_element_type=jnp.float32
        ).astype(jnp.bfloat16)
        row_delta = jnp.sum(
            grad_part.astype(jnp.float32) * attended.astype(jnp.float32), axis=2, keepdims=True
        )
        d_probs = jnp.einsum(
            "nqd,nkd->nqk", grad_part, value_part, preferred_element_type=jnp.float32
        )
        d_scores = (soft_probs * (d_probs - row_delta) * scale_factor).astype(jnp.bfloat16)
        d_query = jnp.einsum(
            "nqk,nkd->nqd", d_scores, key_part, preferred_element_type=jnp.float32
        ).astype(jnp.bfloat16)
        key_terms = jnp.einsum(
            "nqk,nqd->nkd", d_scores, query_part, preferred_element_type=jnp.float32
        ).reshape(group_size * select, BLOCK * head_dim)
        value_terms = jnp.einsum(
            "nqk,nqd->nkd", probs_bf, grad_part, preferred_element_type=jnp.float32
        ).reshape(group_size * select, BLOCK * head_dim)
        owner_map = (owner_rows == chosen[None, :]).astype(jnp.float32)
        key_acc = key_acc + jnp.dot(
            owner_map,
            key_terms,
            precision=lax.Precision.HIGHEST,
            preferred_element_type=jnp.float32,
        )
        value_acc = value_acc + jnp.dot(
            owner_map,
            value_terms,
            precision=lax.Precision.HIGHEST,
            preferred_element_type=jnp.float32,
        )
        return ((key_acc, value_acc), (attended, d_query))

    blank_acc = jnp.zeros((block_count, BLOCK * head_dim), jnp.float32)
    sums, stacked = lax.scan(
        one_group, (blank_acc, blank_acc), jnp.arange(block_count // group_size, dtype=jnp.int32)
    )
    return (
        stacked[0].reshape(seq_len, head_dim),
        stacked[1].reshape(seq_len, head_dim),
        sums[0].reshape(seq_len, head_dim).astype(jnp.bfloat16),
        sums[1].reshape(seq_len, head_dim).astype(jnp.bfloat16),
    )


def general_device(tokens, w_query, w_key, w_value, w_output, grad_out, doc_lengths, block_ids):
    tok_rows = tokens[0]
    cotangent = grad_out[0]
    tok_dev, width = tok_rows.shape
    ctx_size = lax.axis_size("ctx")
    local_heads = HEADS // ctx_size
    head_band = local_heads * HEAD_DIM
    group_rows = (
        lax.all_gather(w_query, "ctx", axis=0, tiled=True),
        lax.all_gather(w_key, "ctx", axis=0, tiled=True),
        lax.all_gather(w_value, "ctx", axis=0, tiled=True),
        lax.all_gather(w_output, "ctx", axis=0, tiled=True),
    )
    pieces = (
        lax.all_gather(group_rows[0], "fsdp", axis=0, tiled=True),
        lax.all_gather(group_rows[1], "fsdp", axis=0, tiled=True),
        lax.all_gather(group_rows[2], "fsdp", axis=0, tiled=True),
        lax.all_gather(group_rows[3], "fsdp", axis=0, tiled=True),
    )
    tok_part = tok_rows
    query_acc = jnp.dot(tok_part, pieces[0], preferred_element_type=jnp.float32)
    key_acc = jnp.dot(tok_part, pieces[1], preferred_element_type=jnp.float32)
    value_acc = jnp.dot(tok_part, pieces[2], preferred_element_type=jnp.float32)
    grad_acc = contract_last(cotangent, pieces[3])
    queries = query_acc.astype(jnp.bfloat16)
    keys_all = key_acc.astype(jnp.bfloat16)
    values_all = value_acc.astype(jnp.bfloat16)
    d_attended = grad_acc.astype(jnp.bfloat16)

    def to_band(matrix):
        return matrix.reshape(tok_dev, ctx_size, head_band)

    received = (
        lax.all_to_all(to_band(queries), "ctx", split_axis=1, concat_axis=0, tiled=True),
        lax.all_to_all(to_band(keys_all), "ctx", split_axis=1, concat_axis=0, tiled=True),
        lax.all_to_all(to_band(values_all), "ctx", split_axis=1, concat_axis=0, tiled=True),
        lax.all_to_all(to_band(d_attended), "ctx", split_axis=1, concat_axis=0, tiled=True),
    )
    query_heads = received[0].reshape(-1, head_band)
    key_heads = received[1].reshape(-1, head_band)
    value_heads = received[2].reshape(-1, head_band)
    grad_heads = received[3].reshape(-1, head_band)
    seq_len = query_heads.shape[0]
    segments = segment_ids(doc_lengths[0], seq_len)
    head_base = lax.axis_index("ctx") * local_heads

    def per_head(head_index, buffers):
        column = head_index * HEAD_DIM

        def columns(matrix):
            return lax.dynamic_slice_in_dim(matrix, column, HEAD_DIM, 1)

        blocks = lax.dynamic_slice_in_dim(block_ids, head_base + head_index, 1, 0)[0]
        results = head_pass(
            columns(query_heads),
            columns(key_heads),
            columns(value_heads),
            columns(grad_heads),
            blocks,
            segments,
        )
        return (
            lax.dynamic_update_slice_in_dim(buffers[0], results[0], column, 1),
            lax.dynamic_update_slice_in_dim(buffers[1], results[1], column, 1),
            lax.dynamic_update_slice_in_dim(buffers[2], results[2], column, 1),
            lax.dynamic_update_slice_in_dim(buffers[3], results[3], column, 1),
        )

    blank_band = jnp.zeros((seq_len, head_band), jnp.bfloat16)
    buffers = lax.fori_loop(
        0, local_heads, per_head, (blank_band, blank_band, blank_band, blank_band)
    )

    def to_rows(matrix):
        return matrix.reshape(seq_len, 1, head_band)

    returned = (
        lax.all_to_all(to_rows(buffers[0]), "ctx", split_axis=0, concat_axis=1, tiled=True),
        lax.all_to_all(to_rows(buffers[1]), "ctx", split_axis=0, concat_axis=1, tiled=True),
        lax.all_to_all(to_rows(buffers[2]), "ctx", split_axis=0, concat_axis=1, tiled=True),
        lax.all_to_all(to_rows(buffers[3]), "ctx", split_axis=0, concat_axis=1, tiled=True),
    )
    attended = returned[0].reshape(tok_dev, width)
    d_query = returned[1].reshape(tok_dev, width)
    d_key = returned[2].reshape(tok_dev, width)
    d_value = returned[3].reshape(tok_dev, width)
    pieces = (
        lax.all_gather(group_rows[0], "fsdp", axis=0, tiled=True),
        lax.all_gather(group_rows[1], "fsdp", axis=0, tiled=True),
        lax.all_gather(group_rows[2], "fsdp", axis=0, tiled=True),
        lax.all_gather(group_rows[3], "fsdp", axis=0, tiled=True),
    )
    out_acc = tok_rows.astype(jnp.float32)
    att_part = attended
    out_acc = out_acc + jnp.dot(att_part, pieces[3], preferred_element_type=jnp.float32)
    update = (
        contract_last(d_query, pieces[0])
        + contract_last(d_key, pieces[1])
        + contract_last(d_value, pieces[2])
    )
    grad_acc = update
    layer_out = out_acc.astype(jnp.bfloat16)
    grad_tokens = (cotangent.astype(jnp.float32) + grad_acc).astype(jnp.bfloat16)
    total_tokens = tok_dev * lax.axis_size("dp") * lax.axis_size("fsdp") * ctx_size
    grad_scale = total_tokens ** (-0.5)
    tok_part = tok_rows
    att_part = attended
    summed = lax.psum_scatter(
        jnp.concatenate(
            [
                contract_first(tok_part, d_query),
                contract_first(tok_part, d_key),
                contract_first(tok_part, d_value),
                contract_first(att_part, cotangent),
            ],
            axis=1,
        )
        * grad_scale,
        ("fsdp", "ctx"),
        scatter_dimension=0,
        tiled=True,
    )
    summed = lax.psum(summed, "dp")
    return (
        layer_out[None],
        grad_tokens[None],
        summed[:, 0:width],
        summed[:, width : 2 * width],
        summed[:, 2 * width : 3 * width],
        summed[:, 3 * width : 4 * width],
    )


def attention_kernel(
    logs_ref, seg_row_ref, seg_col_ref, q_ref, k_ref, v_ref, g_ref,
    att_ref, dq_ref, dk_ref, dv_ref, dk_acc, dv_acc,
):
    seq_len, lanes = q_ref.shape
    heads_here = lanes // HEAD_DIM
    block_count = seq_len // BLOCK
    tile = BLOCK * (2 if block_count % 2 == 0 else 1)
    scale_factor = HEAD_DIM ** (-0.5)
    lane_ids = lax.broadcasted_iota(jnp.int32, (1, lanes), 1) // HEAD_DIM
    keys = k_ref[...]
    values = v_ref[...]
    dk_acc[...] = jnp.zeros_like(dk_acc)
    dv_acc[...] = jnp.zeros_like(dv_acc)
    seg_keys = seg_col_ref[...]
    zero = jnp.zeros((), jnp.bfloat16)

    for part in range(seq_len // tile):
        rows = pl.ds(part * tile, tile)
        query_part = q_ref[rows, :] * jnp.asarray(scale_factor, jnp.bfloat16)
        grad_part = g_ref[rows, :]
        live = seg_keys == seg_row_ref[:, rows]
        att_sum = jnp.zeros((tile, lanes), jnp.float32)
        dq_sum = jnp.zeros((tile, lanes), jnp.float32)
        for head in range(heads_here):
            mine = lane_ids == head
            q_head = jnp.where(mine, query_part, zero)
            g_head = jnp.where(mine, grad_part, zero)
            scores = contract_last(keys, q_head)
            bias = jnp.broadcast_to(
                logs_ref[head, :, rows][:, None, :], (block_count, BLOCK, tile)
            ).reshape(seq_len, tile)
            scores = jnp.where(live, scores + bias, -1e30)
            top_score = jnp.max(scores, axis=0, keepdims=True)
            weights = jnp.exp(scores - top_score)
            inverse = 1.0 / jnp.sum(weights, axis=0, keepdims=True)
            probs = weights * inverse
            d_probs = contract_last(values, g_head)
            row_delta = jnp.sum(probs * d_probs, axis=0, keepdims=True)
            probs_bf = probs.astype(jnp.bfloat16)
            d_scores = (probs * (d_probs - row_delta)).astype(jnp.bfloat16)
            att_sum = jnp.where(mine, contract_first(probs_bf, values), att_sum)
            dq_sum = jnp.where(mine, contract_first(d_scores, keys), dq_sum)
            dv_acc[...] += jnp.dot(probs_bf, g_head, preferred_element_type=jnp.float32)
            dk_acc[...] += jnp.dot(d_scores, q_head, preferred_element_type=jnp.float32)
        att_ref[rows, :] = att_sum.astype(jnp.bfloat16)
        dq_ref[rows, :] = (dq_sum * scale_factor).astype(jnp.bfloat16)
    dk_ref[...] = dk_acc[...].astype(jnp.bfloat16)
    dv_ref[...] = dv_acc[...].astype(jnp.bfloat16)


def attention(queries, keys, values, grads, logs, segments, stripe):
    seq_len, band = queries.shape
    heads_here = stripe // HEAD_DIM
    block_count = logs.shape[1]
    whole = pl.BlockSpec((seq_len, stripe), lambda i: (0, i))
    return pl.pallas_call(
        attention_kernel,
        grid=(band // stripe,),
        out_shape=[jax.ShapeDtypeStruct((seq_len, band), jnp.bfloat16)] * 4,
        in_specs=[
            pl.BlockSpec((heads_here, block_count, seq_len), lambda i: (i, 0, 0)),
            pl.BlockSpec((1, seq_len), lambda i: (0, 0)),
            pl.BlockSpec((seq_len, 1), lambda i: (0, 0)),
            whole, whole, whole, whole,
        ],
        out_specs=[whole] * 4,
        scratch_shapes=[pltpu.VMEM((seq_len, stripe), jnp.float32)] * 2,
        compiler_params=pltpu.CompilerParams(vmem_limit_bytes=48 * 1024 * 1024),
        name="attention",
    )(logs, segments[None, :], segments[:, None], queries, keys, values, grads)


def block_logs(blocks, seq_len):
    block_count = blocks.shape[1]
    ids = jnp.arange(block_count, dtype=jnp.int32)
    counts = jnp.sum((blocks[:, None, :, :] == ids[None, :, None, None]).astype(jnp.float32), 3)
    logs = jnp.where(counts > 0, jnp.log(jnp.maximum(counts, 1.0)), -1e30)
    return jnp.repeat(logs, seq_len // block_count, axis=2)


def striped_device(tokens, w_query, w_key, w_value, w_output, grad_out, doc_lengths, block_ids):
    tok_rows = tokens[0]
    cotangent = grad_out[0]
    tok_dev, width = tok_rows.shape
    rows = w_query.shape[0]
    dp_size, fsdp_size = lax.axis_size("dp"), lax.axis_size("fsdp")
    ctx_size = 2
    me = lax.axis_index("ctx")
    swap = [(0, 1), (1, 0)]
    band = fsdp_size * rows
    seq_len = tok_dev * ctx_size
    share = rows // dp_size

    def other(matrix):
        return lax.ppermute(matrix, "ctx", swap)

    def ordered(own, peer):
        first = me == 0
        return jnp.stack([jnp.where(first, own, peer), jnp.where(first, peer, own)])

    tok_peer = other(tok_rows)
    cot_peer = other(cotangent)

    start = lax.axis_index("dp") * share

    def my_share(matrix):
        return lax.dynamic_slice_in_dim(matrix, start, share, 0)

    qkv = jnp.stack([my_share(w_query), my_share(w_key), my_share(w_value)], axis=1)
    qkv = qkv.reshape(share, 3, fsdp_size, ctx_size, rows)
    kept = lax.dynamic_index_in_dim(qkv, me, 3, False).reshape(share, 3 * band)
    sent = lax.dynamic_index_in_dim(qkv, 1 - me, 3, False).reshape(share, 3 * band)
    qkv = ordered(kept, other(sent))
    out_share = my_share(w_output).reshape(share, ctx_size, width // 2).transpose(1, 0, 2)
    packed = jnp.concatenate([qkv, out_share], axis=2)
    gathered = lax.all_gather(packed, ("fsdp", "dp"), axis=0, tiled=False)
    gathered = gathered.reshape(fsdp_size, dp_size, ctx_size, share, 3 * band + width // 2)
    w_qkv = gathered[..., : 3 * band].transpose(0, 2, 1, 3, 4).reshape(width, 3 * band)
    w_out = gathered[..., 3 * band :].transpose(0, 1, 3, 2, 4).reshape(band, width)

    tok_all = ordered(tok_rows, tok_peer).reshape(seq_len, width)
    cot_all = ordered(cotangent, cot_peer).reshape(seq_len, width)
    queries = jnp.dot(
        tok_all, w_qkv[:, :band], preferred_element_type=jnp.float32
    ).astype(jnp.bfloat16)
    keys = jnp.dot(
        tok_all, w_qkv[:, band : 2 * band], preferred_element_type=jnp.float32
    ).astype(jnp.bfloat16)
    values = jnp.dot(
        tok_all, w_qkv[:, 2 * band :], preferred_element_type=jnp.float32
    ).astype(jnp.bfloat16)
    d_attended = contract_last(cot_all, w_out).astype(jnp.bfloat16)

    segments = segment_ids(doc_lengths[0], seq_len)
    stripe_heads = rows // HEAD_DIM
    my_blocks = lax.dynamic_index_in_dim(
        block_ids.reshape((fsdp_size, ctx_size, stripe_heads) + block_ids.shape[1:]), me, 1, False
    ).reshape((fsdp_size * stripe_heads,) + block_ids.shape[1:])
    logs = block_logs(my_blocks, seq_len)
    attended, d_query, d_key, d_value = attention(
        queries, keys, values, d_attended, logs, segments, rows
    )
    d_qkv = jnp.concatenate([d_query, d_key, d_value], axis=1)

    total_tokens = tok_dev * dp_size * fsdp_size * ctx_size
    grad_scale = total_tokens ** (-0.5)
    g_qkv = (contract_first(tok_all, d_qkv) * grad_scale).astype(jnp.bfloat16)
    g_out = (contract_first(attended, cot_all) * grad_scale).astype(jnp.bfloat16)
    g_qkv = g_qkv.reshape(fsdp_size, ctx_size, dp_size, share, 3 * band).transpose(2, 0, 1, 3, 4)
    g_out = g_out.reshape(fsdp_size, dp_size, share, ctx_size, width // 2).transpose(1, 0, 3, 2, 4)
    partial = jnp.concatenate([g_qkv, g_out], axis=4)
    out_part = jnp.dot(attended, w_out, preferred_element_type=jnp.float32)
    tok_part = contract_last(d_qkv, w_qkv)
    out_part = out_part.reshape(ctx_size, tok_dev, width)
    tok_part = tok_part.reshape(ctx_size, tok_dev, width)

    def pick(matrix, index):
        return lax.dynamic_index_in_dim(matrix, index, 0, False)

    out_give = pick(out_part, 1 - me).astype(jnp.bfloat16)
    tok_give = pick(tok_part, 1 - me).astype(jnp.bfloat16)
    summed = lax.psum_scatter(partial, "dp", scatter_dimension=0, tiled=False)
    out_sent = other(out_give)
    tok_sent = other(tok_give)
    summed, out_sent, tok_sent = lax.optimization_barrier((summed, out_sent, tok_sent))
    summed = lax.psum_scatter(summed, "fsdp", scatter_dimension=0, tiled=False)
    s_qkv = summed[..., : 3 * band]
    kept = lax.dynamic_index_in_dim(s_qkv, me, 0, False)
    sent = lax.dynamic_index_in_dim(s_qkv, 1 - me, 0, False)
    final = jnp.concatenate([ordered(kept, other(sent)), summed[..., 3 * band :]], axis=2)
    final = lax.all_gather(final, "dp", axis=0, tiled=False)

    def full_rows(which):
        block = final[..., which * band : (which + 1) * band]
        block = block.reshape(dp_size, ctx_size, share, fsdp_size, rows)
        return block.transpose(0, 2, 3, 1, 4).reshape(rows, width).astype(jnp.float32)

    f_out = final[..., 3 * band :].transpose(0, 2, 1, 3).reshape(rows, width).astype(jnp.float32)

    layer_out = tok_rows.astype(jnp.float32) + pick(out_part, me) + out_sent.astype(jnp.float32)
    grad_tokens = cotangent.astype(jnp.float32) + pick(tok_part, me) + tok_sent.astype(jnp.float32)
    return (
        layer_out.astype(jnp.bfloat16)[None],
        grad_tokens.astype(jnp.bfloat16)[None],
        full_rows(0),
        full_rows(1),
        full_rows(2),
        f_out,
    )


def per_device(tokens, w_query, w_key, w_value, w_output, grad_out, doc_lengths, block_ids):
    rows = w_query.shape[0]
    dp_size = lax.axis_size("dp")
    striped = (
        lax.axis_size("ctx") == 2
        and rows % 128 == 0
        and rows % HEAD_DIM == 0
        and rows % (dp_size * 16) == 0
    )
    body = striped_device if striped else general_device
    return body(tokens, w_query, w_key, w_value, w_output, grad_out, doc_lengths, block_ids)


def solution(mesh):
    in_specs = (
        P(("dp", "fsdp"), "ctx", None),
        P(("fsdp", "ctx"), None),
        P(("fsdp", "ctx"), None),
        P(("fsdp", "ctx"), None),
        P(("fsdp", "ctx"), None),
        P(("dp", "fsdp"), "ctx", None),
        P(("dp", "fsdp"), None),
        P(),
    )
    out_specs = (
        P(("dp", "fsdp"), "ctx", None),
        P(("dp", "fsdp"), "ctx", None),
        P(("fsdp", "ctx"), None),
        P(("fsdp", "ctx"), None),
        P(("fsdp", "ctx"), None),
        P(("fsdp", "ctx"), None),
    )
    return jax.shard_map(
        per_device, mesh=mesh, in_specs=in_specs, out_specs=out_specs, check_vma=False
    )
```

```python
import math

import jax
import jax.numpy as jnp
from jax import lax
from jax.experimental import pallas as pl
from jax.experimental.pallas import tpu as pltpu
from jax.sharding import PartitionSpec as P

HEADS = 16
HEAD_DIM = 64
BLOCK = 128


def contract_last(left_rows, right_rows):
    return lax.dot_general(
        left_rows, right_rows, (((1,), (1,)), ((), ())), preferred_element_type=jnp.float32
    )


def contract_first(left_rows, right_rows):
    return lax.dot_general(
        left_rows, right_rows, (((0,), (0,)), ((), ())), preferred_element_type=jnp.float32
    )


def segment_ids(lengths, count):
    doc_ends = jnp.cumsum(lengths)
    places = lax.broadcasted_iota(jnp.int32, (lengths.shape[0], count), 1)
    return jnp.sum((places >= doc_ends[:, None]).astype(jnp.int32), axis=0)


def head_pass(queries, keys_in, values_in, grads_in, blocks, segments):
    seq_len, head_dim = queries.shape
    block_count = seq_len // BLOCK
    select = blocks.shape[1]
    group_size = math.gcd(block_count, max(1, 512 // BLOCK))
    scale_factor = head_dim ** (-0.5)
    query_blocks = queries.reshape(block_count, BLOCK, head_dim)
    key_blocks = keys_in.reshape(block_count, BLOCK, head_dim)
    value_blocks = values_in.reshape(block_count, BLOCK, head_dim)
    grad_blocks = grads_in.reshape(block_count, BLOCK, head_dim)
    seg_blocks = segments.reshape(block_count, BLOCK)
    owner_rows = lax.broadcasted_iota(jnp.int32, (block_count, group_size * select), 0)

    def one_group(carried, group_index):
        key_acc, value_acc = carried
        first_block = group_index * group_size
        chosen = lax.dynamic_slice_in_dim(blocks, first_block, group_size, 0).reshape(-1)
        query_part = lax.dynamic_slice_in_dim(query_blocks, first_block, group_size, 0)
        grad_part = lax.dynamic_slice_in_dim(grad_blocks, first_block, group_size, 0)
        query_segs = lax.dynamic_slice_in_dim(seg_blocks, first_block, group_size, 0)
        key_part = key_blocks[chosen].reshape(group_size, select * BLOCK, head_dim)
        value_part = value_blocks[chosen].reshape(group_size, select * BLOCK, head_dim)
        key_segs = seg_blocks[chosen].reshape(group_size, select * BLOCK)
        live_mask = query_segs[:, :, None] == key_segs[:, None, :]
        scores = (
            jnp.einsum("nqd,nkd->nqk", query_part, key_part, preferred_element_type=jnp.float32)
            * scale_factor
        )
        scores = jnp.where(live_mask, scores, -1e30)
        top_score = jnp.max(scores, axis=2, keepdims=True)
        weights = jnp.where(live_mask, jnp.exp(scores - top_score), 0.0)
        soft_probs = weights / jnp.sum(weights, axis=2, keepdims=True)
        probs_bf = soft_probs.astype(jnp.bfloat16)
        attended = jnp.einsum(
            "nqk,nkd->nqd", probs_bf, value_part, preferred_element_type=jnp.float32
        ).astype(jnp.bfloat16)
        row_delta = jnp.sum(
            grad_part.astype(jnp.float32) * attended.astype(jnp.float32), axis=2, keepdims=True
        )
        d_probs = jnp.einsum(
            "nqd,nkd->nqk", grad_part, value_part, preferred_element_type=jnp.float32
        )
        d_scores = (soft_probs * (d_probs - row_delta) * scale_factor).astype(jnp.bfloat16)
        d_query = jnp.einsum(
            "nqk,nkd->nqd", d_scores, key_part, preferred_element_type=jnp.float32
        ).astype(jnp.bfloat16)
        key_terms = jnp.einsum(
            "nqk,nqd->nkd", d_scores, query_part, preferred_element_type=jnp.float32
        ).reshape(group_size * select, BLOCK * head_dim)
        value_terms = jnp.einsum(
            "nqk,nqd->nkd", probs_bf, grad_part, preferred_element_type=jnp.float32
        ).reshape(group_size * select, BLOCK * head_dim)
        owner_map = (owner_rows == chosen[None, :]).astype(jnp.float32)
        key_acc = key_acc + jnp.dot(
            owner_map,
            key_terms,
            precision=lax.Precision.HIGHEST,
            preferred_element_type=jnp.float32,
        )
        value_acc = value_acc + jnp.dot(
            owner_map,
            value_terms,
            precision=lax.Precision.HIGHEST,
            preferred_element_type=jnp.float32,
        )
        return ((key_acc, value_acc), (attended, d_query))

    blank_acc = jnp.zeros((block_count, BLOCK * head_dim), jnp.float32)
    sums, stacked = lax.scan(
        one_group, (blank_acc, blank_acc), jnp.arange(block_count // group_size, dtype=jnp.int32)
    )
    return (
        stacked[0].reshape(seq_len, head_dim),
        stacked[1].reshape(seq_len, head_dim),
        sums[0].reshape(seq_len, head_dim).astype(jnp.bfloat16),
        sums[1].reshape(seq_len, head_dim).astype(jnp.bfloat16),
    )


def general_device(tokens, w_query, w_key, w_value, w_output, grad_out, doc_lengths, block_ids):
    tok_rows = tokens[0]
    cotangent = grad_out[0]
    tok_dev, width = tok_rows.shape
    ctx_size = lax.axis_size("ctx")
    local_heads = HEADS // ctx_size
    head_band = local_heads * HEAD_DIM
    group_rows = (
        lax.all_gather(w_query, "ctx", axis=0, tiled=True),
        lax.all_gather(w_key, "ctx", axis=0, tiled=True),
        lax.all_gather(w_value, "ctx", axis=0, tiled=True),
        lax.all_gather(w_output, "ctx", axis=0, tiled=True),
    )
    pieces = (
        lax.all_gather(group_rows[0], "fsdp", axis=0, tiled=True),
        lax.all_gather(group_rows[1], "fsdp", axis=0, tiled=True),
        lax.all_gather(group_rows[2], "fsdp", axis=0, tiled=True),
        lax.all_gather(group_rows[3], "fsdp", axis=0, tiled=True),
    )
    tok_part = tok_rows
    query_acc = jnp.dot(tok_part, pieces[0], preferred_element_type=jnp.float32)
    key_acc = jnp.dot(tok_part, pieces[1], preferred_element_type=jnp.float32)
    value_acc = jnp.dot(tok_part, pieces[2], preferred_element_type=jnp.float32)
    grad_acc = contract_last(cotangent, pieces[3])
    queries = query_acc.astype(jnp.bfloat16)
    keys_all = key_acc.astype(jnp.bfloat16)
    values_all = value_acc.astype(jnp.bfloat16)
    d_attended = grad_acc.astype(jnp.bfloat16)

    def to_band(matrix):
        return matrix.reshape(tok_dev, ctx_size, head_band)

    received = (
        lax.all_to_all(to_band(queries), "ctx", split_axis=1, concat_axis=0, tiled=True),
        lax.all_to_all(to_band(keys_all), "ctx", split_axis=1, concat_axis=0, tiled=True),
        lax.all_to_all(to_band(values_all), "ctx", split_axis=1, concat_axis=0, tiled=True),
        lax.all_to_all(to_band(d_attended), "ctx", split_axis=1, concat_axis=0, tiled=True),
    )
    query_heads = received[0].reshape(-1, head_band)
    key_heads = received[1].reshape(-1, head_band)
    value_heads = received[2].reshape(-1, head_band)
    grad_heads = received[3].reshape(-1, head_band)
    seq_len = query_heads.shape[0]
    segments = segment_ids(doc_lengths[0], seq_len)
    head_base = lax.axis_index("ctx") * local_heads

    def per_head(head_index, buffers):
        column = head_index * HEAD_DIM

        def columns(matrix):
            return lax.dynamic_slice_in_dim(matrix, column, HEAD_DIM, 1)

        blocks = lax.dynamic_slice_in_dim(block_ids, head_base + head_index, 1, 0)[0]
        results = head_pass(
            columns(query_heads),
            columns(key_heads),
            columns(value_heads),
            columns(grad_heads),
            blocks,
            segments,
        )
        return (
            lax.dynamic_update_slice_in_dim(buffers[0], results[0], column, 1),
            lax.dynamic_update_slice_in_dim(buffers[1], results[1], column, 1),
            lax.dynamic_update_slice_in_dim(buffers[2], results[2], column, 1),
            lax.dynamic_update_slice_in_dim(buffers[3], results[3], column, 1),
        )

    blank_band = jnp.zeros((seq_len, head_band), jnp.bfloat16)
    buffers = lax.fori_loop(
        0, local_heads, per_head, (blank_band, blank_band, blank_band, blank_band)
    )

    def to_rows(matrix):
        return matrix.reshape(seq_len, 1, head_band)

    returned = (
        lax.all_to_all(to_rows(buffers[0]), "ctx", split_axis=0, concat_axis=1, tiled=True),
        lax.all_to_all(to_rows(buffers[1]), "ctx", split_axis=0, concat_axis=1, tiled=True),
        lax.all_to_all(to_rows(buffers[2]), "ctx", split_axis=0, concat_axis=1, tiled=True),
        lax.all_to_all(to_rows(buffers[3]), "ctx", split_axis=0, concat_axis=1, tiled=True),
    )
    attended = returned[0].reshape(tok_dev, width)
    d_query = returned[1].reshape(tok_dev, width)
    d_key = returned[2].reshape(tok_dev, width)
    d_value = returned[3].reshape(tok_dev, width)
    pieces = (
        lax.all_gather(group_rows[0], "fsdp", axis=0, tiled=True),
        lax.all_gather(group_rows[1], "fsdp", axis=0, tiled=True),
        lax.all_gather(group_rows[2], "fsdp", axis=0, tiled=True),
        lax.all_gather(group_rows[3], "fsdp", axis=0, tiled=True),
    )
    out_acc = tok_rows.astype(jnp.float32)
    att_part = attended
    out_acc = out_acc + jnp.dot(att_part, pieces[3], preferred_element_type=jnp.float32)
    update = (
        contract_last(d_query, pieces[0])
        + contract_last(d_key, pieces[1])
        + contract_last(d_value, pieces[2])
    )
    grad_acc = update
    layer_out = out_acc.astype(jnp.bfloat16)
    grad_tokens = (cotangent.astype(jnp.float32) + grad_acc).astype(jnp.bfloat16)
    total_tokens = tok_dev * lax.axis_size("dp") * lax.axis_size("fsdp") * ctx_size
    grad_scale = total_tokens ** (-0.5)
    tok_part = tok_rows
    att_part = attended
    summed = lax.psum_scatter(
        jnp.concatenate(
            [
                contract_first(tok_part, d_query),
                contract_first(tok_part, d_key),
                contract_first(tok_part, d_value),
                contract_first(att_part, cotangent),
            ],
            axis=1,
        )
        * grad_scale,
        ("fsdp", "ctx"),
        scatter_dimension=0,
        tiled=True,
    )
    summed = lax.psum(summed, "dp")
    return (
        layer_out[None],
        grad_tokens[None],
        summed[:, 0:width],
        summed[:, width : 2 * width],
        summed[:, 2 * width : 3 * width],
        summed[:, 3 * width : 4 * width],
    )


def attention_kernel(
    logs_ref, seg_row_ref, seg_col_ref, q_ref, k_ref, v_ref, g_ref,
    att_ref, dq_ref, dk_ref, dv_ref, dk_acc, dv_acc,
):
    seq_len, lanes = q_ref.shape
    heads_here = lanes // HEAD_DIM
    block_count = seq_len // BLOCK
    tile = BLOCK * (2 if block_count % 2 == 0 else 1)
    scale_factor = HEAD_DIM ** (-0.5)
    lane_ids = lax.broadcasted_iota(jnp.int32, (1, lanes), 1) // HEAD_DIM
    keys = k_ref[...]
    values = v_ref[...]
    dk_acc[...] = jnp.zeros_like(dk_acc)
    dv_acc[...] = jnp.zeros_like(dv_acc)
    seg_keys = seg_col_ref[...]
    zero = jnp.zeros((), jnp.bfloat16)

    for part in range(seq_len // tile):
        rows = pl.ds(part * tile, tile)
        query_part = q_ref[rows, :] * jnp.asarray(scale_factor, jnp.bfloat16)
        grad_part = g_ref[rows, :]
        live = seg_keys == seg_row_ref[:, rows]
        att_sum = jnp.zeros((tile, lanes), jnp.float32)
        dq_sum = jnp.zeros((tile, lanes), jnp.float32)
        for head in range(heads_here):
            mine = lane_ids == head
            q_head = jnp.where(mine, query_part, zero)
            g_head = jnp.where(mine, grad_part, zero)
            scores = contract_last(keys, q_head)
            bias = jnp.broadcast_to(
                logs_ref[head, :, rows][:, None, :], (block_count, BLOCK, tile)
            ).reshape(seq_len, tile)
            scores = jnp.where(live, scores + bias, -1e30)
            top_score = jnp.max(scores, axis=0, keepdims=True)
            weights = jnp.exp(scores - top_score)
            inverse = 1.0 / jnp.sum(weights, axis=0, keepdims=True)
            probs = weights * inverse
            d_probs = contract_last(values, g_head)
            row_delta = jnp.sum(probs * d_probs, axis=0, keepdims=True)
            probs_bf = probs.astype(jnp.bfloat16)
            d_scores = (probs * (d_probs - row_delta)).astype(jnp.bfloat16)
            att_sum = jnp.where(mine, contract_first(probs_bf, values), att_sum)
            dq_sum = jnp.where(mine, contract_first(d_scores, keys), dq_sum)
            dv_acc[...] += jnp.dot(probs_bf, g_head, preferred_element_type=jnp.float32)
            dk_acc[...] += jnp.dot(d_scores, q_head, preferred_element_type=jnp.float32)
        att_ref[rows, :] = att_sum.astype(jnp.bfloat16)
        dq_ref[rows, :] = (dq_sum * scale_factor).astype(jnp.bfloat16)
    dk_ref[...] = dk_acc[...].astype(jnp.bfloat16)
    dv_ref[...] = dv_acc[...].astype(jnp.bfloat16)


def attention(queries, keys, values, grads, logs, segments, stripe):
    seq_len, band = queries.shape
    heads_here = stripe // HEAD_DIM
    block_count = logs.shape[1]
    whole = pl.BlockSpec((seq_len, stripe), lambda i: (0, i))
    return pl.pallas_call(
        attention_kernel,
        grid=(band // stripe,),
        out_shape=[jax.ShapeDtypeStruct((seq_len, band), jnp.bfloat16)] * 4,
        in_specs=[
            pl.BlockSpec((heads_here, block_count, seq_len), lambda i: (i, 0, 0)),
            pl.BlockSpec((1, seq_len), lambda i: (0, 0)),
            pl.BlockSpec((seq_len, 1), lambda i: (0, 0)),
            whole, whole, whole, whole,
        ],
        out_specs=[whole] * 4,
        scratch_shapes=[pltpu.VMEM((seq_len, stripe), jnp.float32)] * 2,
        compiler_params=pltpu.CompilerParams(vmem_limit_bytes=48 * 1024 * 1024),
        name="attention",
    )(logs, segments[None, :], segments[:, None], queries, keys, values, grads)


def block_logs(blocks, seq_len):
    block_count = blocks.shape[1]
    ids = jnp.arange(block_count, dtype=jnp.int32)
    counts = jnp.sum((blocks[:, None, :, :] == ids[None, :, None, None]).astype(jnp.float32), 3)
    logs = jnp.where(counts > 0, jnp.log(jnp.maximum(counts, 1.0)), -1e30)
    return jnp.repeat(logs, seq_len // block_count, axis=2)


def striped_device(tokens, w_query, w_key, w_value, w_output, grad_out, doc_lengths, block_ids):
    tok_rows = tokens[0]
    cotangent = grad_out[0]
    tok_dev, width = tok_rows.shape
    rows = w_query.shape[0]
    dp_size, fsdp_size = lax.axis_size("dp"), lax.axis_size("fsdp")
    ctx_size = 2
    me = lax.axis_index("ctx")
    swap = [(0, 1), (1, 0)]
    band = fsdp_size * rows
    seq_len = tok_dev * ctx_size
    share = rows // dp_size

    def other(matrix):
        return lax.ppermute(matrix, "ctx", swap)

    dp_bits, fsdp_bits = dp_size.bit_length() - 1, fsdp_size.bit_length() - 1

    def flip(matrix, axis, size, bit):
        return lax.ppermute(matrix, axis, [(i, i ^ (1 << bit)) for i in range(size)])

    def join(block, axis, size, bit):
        peer = flip(block, axis, size, bit)
        low = (lax.axis_index(axis) >> bit) % 2 == 0
        return jnp.stack([jnp.where(low, block, peer), jnp.where(low, peer, block)])

    def fold(block, axis, size, bit):
        side = (lax.axis_index(axis) >> bit) % 2
        given = flip(lax.dynamic_index_in_dim(block, 1 - side, 0, False), axis, size, bit)
        kept = lax.dynamic_index_in_dim(block, side, 0, False)
        return (kept.astype(jnp.float32) + given.astype(jnp.float32)).astype(jnp.bfloat16)

    def ordered(own, peer):
        first = me == 0
        return jnp.stack([jnp.where(first, own, peer), jnp.where(first, peer, own)])

    tok_peer = other(tok_rows)
    cot_peer = other(cotangent)

    start = lax.axis_index("dp") * share

    def my_share(matrix):
        return lax.dynamic_slice_in_dim(matrix, start, share, 0)

    qkv = jnp.stack([my_share(w_query), my_share(w_key), my_share(w_value)], axis=1)
    qkv = qkv.reshape(share, 3, fsdp_size, ctx_size, rows)
    kept = lax.dynamic_index_in_dim(qkv, me, 3, False).reshape(share, 3 * band)
    sent = lax.dynamic_index_in_dim(qkv, 1 - me, 3, False).reshape(share, 3 * band)
    qkv = ordered(kept, other(sent))
    out_share = my_share(w_output).reshape(share, ctx_size, width // 2).transpose(1, 0, 2)

    def spread(block):
        for bit in reversed(range(fsdp_bits)):
            block = join(block, "fsdp", fsdp_size, bit)
        for bit in reversed(range(dp_bits)):
            block = join(block, "dp", dp_size, bit)
        block = block.reshape((2,) * (dp_bits + fsdp_bits) + block.shape[-3:])
        dp_dims = tuple(reversed(range(dp_bits)))
        fsdp_dims = tuple(dp_bits + d for d in reversed(range(fsdp_bits)))
        last = dp_bits + fsdp_bits
        return block, fsdp_dims, dp_dims, last

    qk_block, fsdp_dims, dp_dims, last = spread(qkv[..., : 2 * band])
    vo_block = spread(jnp.concatenate([qkv[..., 2 * band :], out_share], axis=2))[0]
    row_order = fsdp_dims + (last,) + dp_dims + (last + 1, last + 2)
    out_order = fsdp_dims + dp_dims + (last + 1, last, last + 2)
    w_qk = qk_block.transpose(row_order).reshape(width, 2 * band)
    w_value_all = vo_block[..., :band].transpose(row_order).reshape(width, band)
    w_out = vo_block[..., band:].transpose(out_order).reshape(band, width)

    tok_all = ordered(tok_rows, tok_peer).reshape(seq_len, width)
    cot_all = ordered(cotangent, cot_peer).reshape(seq_len, width)
    queries = jnp.dot(
        tok_all, w_qk[:, :band], preferred_element_type=jnp.float32
    ).astype(jnp.bfloat16)
    keys = jnp.dot(
        tok_all, w_qk[:, band:], preferred_element_type=jnp.float32
    ).astype(jnp.bfloat16)
    values = jnp.dot(
        tok_all, w_value_all, preferred_element_type=jnp.float32
    ).astype(jnp.bfloat16)
    d_attended = contract_last(cot_all, w_out).astype(jnp.bfloat16)

    segments = segment_ids(doc_lengths[0], seq_len)
    stripe_heads = rows // HEAD_DIM
    my_blocks = lax.dynamic_index_in_dim(
        block_ids.reshape((fsdp_size, ctx_size, stripe_heads) + block_ids.shape[1:]), me, 1, False
    ).reshape((fsdp_size * stripe_heads,) + block_ids.shape[1:])
    logs = block_logs(my_blocks, seq_len)
    attended, d_query, d_key, d_value = attention(
        queries, keys, values, d_attended, logs, segments, rows
    )
    d_qk = jnp.concatenate([d_query, d_key], axis=1)

    total_tokens = tok_dev * dp_size * fsdp_size * ctx_size
    grad_scale = total_tokens ** (-0.5)
    halves = (2,) * fsdp_bits, (2,) * dp_bits

    def scaled(product):
        return (product * grad_scale).astype(jnp.bfloat16)

    def row_parts(matrix):
        columns = matrix.shape[1]
        parts = matrix.reshape(halves[0] + (ctx_size,) + halves[1] + (share, columns))
        dp_dims = tuple(fsdp_bits + 1 + d for d in reversed(range(dp_bits)))
        fsdp_dims = tuple(reversed(range(fsdp_bits)))
        rest = dp_bits + fsdp_bits + 1
        return parts.transpose(dp_dims + fsdp_dims + (fsdp_bits, rest, rest + 1))

    g_out = scaled(contract_first(attended, cot_all))
    out_parts = g_out.reshape(halves[0] + halves[1] + (share, ctx_size, width // 2))
    rest = dp_bits + fsdp_bits
    out_parts = out_parts.transpose(
        tuple(reversed(range(rest)))[:dp_bits]
        + tuple(reversed(range(fsdp_bits)))
        + (rest + 1, rest, rest + 2)
    )
    vo_sum = jnp.concatenate(
        [row_parts(scaled(contract_first(tok_all, d_value))), out_parts], axis=-1
    )
    qk_sum = row_parts(scaled(contract_first(tok_all, d_qk)))
    for bit in range(dp_bits):
        vo_sum = fold(vo_sum, "dp", dp_size, bit)
        qk_sum = fold(qk_sum, "dp", dp_size, bit)
    out_part = jnp.dot(attended, w_out, preferred_element_type=jnp.float32)
    tok_part = contract_last(d_qk, w_qk) + contract_last(d_value, w_value_all)
    out_part = out_part.reshape(ctx_size, tok_dev, width)
    tok_part = tok_part.reshape(ctx_size, tok_dev, width)

    def pick(matrix, index):
        return lax.dynamic_index_in_dim(matrix, index, 0, False)

    out_give = pick(out_part, 1 - me).astype(jnp.bfloat16)
    tok_give = pick(tok_part, 1 - me).astype(jnp.bfloat16)
    vo_sum, out_give, tok_give = lax.optimization_barrier((vo_sum, out_give, tok_give))
    out_sent = other(out_give)
    tok_sent = other(tok_give)
    for bit in range(fsdp_bits):
        vo_sum = fold(vo_sum, "fsdp", fsdp_size, bit)
        qk_sum = fold(qk_sum, "fsdp", fsdp_size, bit)

    def over_ctx(matrix):
        kept = lax.dynamic_index_in_dim(matrix, me, 0, False)
        sent = lax.dynamic_index_in_dim(matrix, 1 - me, 0, False)
        return ordered(kept, other(sent))

    def over_dp(block):
        for bit in reversed(range(dp_bits)):
            block = join(block, "dp", dp_size, bit)
        dims = tuple(reversed(range(dp_bits))) + tuple(range(dp_bits, block.ndim))
        return block.transpose(dims).reshape((dp_size,) + block.shape[dp_bits:])

    vo_final = over_dp(
        jnp.concatenate([over_ctx(vo_sum[..., :band]), vo_sum[..., band:]], axis=2)
    )
    qk_final = over_dp(over_ctx(qk_sum))

    def full_rows(block):
        block = block.reshape(dp_size, ctx_size, share, fsdp_size, rows)
        return block.transpose(0, 2, 3, 1, 4).reshape(rows, width).astype(jnp.float32)

    f_out = vo_final[..., band:].transpose(0, 2, 1, 3).reshape(rows, width).astype(jnp.float32)

    layer_out = tok_rows.astype(jnp.float32) + pick(out_part, me) + out_sent.astype(jnp.float32)
    grad_tokens = cotangent.astype(jnp.float32) + pick(tok_part, me) + tok_sent.astype(jnp.float32)
    return (
        layer_out.astype(jnp.bfloat16)[None],
        grad_tokens.astype(jnp.bfloat16)[None],
        full_rows(qk_final[..., :band]),
        full_rows(qk_final[..., band:]),
        full_rows(vo_final[..., :band]),
        f_out,
    )


def per_device(tokens, w_query, w_key, w_value, w_output, grad_out, doc_lengths, block_ids):
    rows = w_query.shape[0]
    dp_size, fsdp_size = lax.axis_size("dp"), lax.axis_size("fsdp")
    striped = (
        lax.axis_size("ctx") == 2
        and dp_size & (dp_size - 1) == 0
        and fsdp_size & (fsdp_size - 1) == 0
        and rows % 128 == 0
        and rows % HEAD_DIM == 0
        and rows % (dp_size * 16) == 0
    )
    body = striped_device if striped else general_device
    return body(tokens, w_query, w_key, w_value, w_output, grad_out, doc_lengths, block_ids)


def solution(mesh):
    in_specs = (
        P(("dp", "fsdp"), "ctx", None),
        P(("fsdp", "ctx"), None),
        P(("fsdp", "ctx"), None),
        P(("fsdp", "ctx"), None),
        P(("fsdp", "ctx"), None),
        P(("dp", "fsdp"), "ctx", None),
        P(("dp", "fsdp"), None),
        P(),
    )
    out_specs = (
        P(("dp", "fsdp"), "ctx", None),
        P(("dp", "fsdp"), "ctx", None),
        P(("fsdp", "ctx"), None),
        P(("fsdp", "ctx"), None),
        P(("fsdp", "ctx"), None),
        P(("fsdp", "ctx"), None),
    )
    return jax.shard_map(
        per_device, mesh=mesh, in_specs=in_specs, out_specs=out_specs, check_vma=False
    )
```

```python
import math

import jax
import jax.numpy as jnp
from jax import lax
from jax.experimental import pallas as pl
from jax.experimental.pallas import tpu as pltpu
from jax.sharding import PartitionSpec as P

HEADS = 16
HEAD_DIM = 64
BLOCK = 128


def contract_last(left_rows, right_rows):
    return lax.dot_general(
        left_rows, right_rows, (((1,), (1,)), ((), ())), preferred_element_type=jnp.float32
    )


def contract_first(left_rows, right_rows):
    return lax.dot_general(
        left_rows, right_rows, (((0,), (0,)), ((), ())), preferred_element_type=jnp.float32
    )


def segment_ids(lengths, count):
    doc_ends = jnp.cumsum(lengths)
    places = lax.broadcasted_iota(jnp.int32, (lengths.shape[0], count), 1)
    return jnp.sum((places >= doc_ends[:, None]).astype(jnp.int32), axis=0)


def head_pass(queries, keys_in, values_in, grads_in, blocks, segments):
    seq_len, head_dim = queries.shape
    block_count = seq_len // BLOCK
    select = blocks.shape[1]
    group_size = math.gcd(block_count, max(1, 512 // BLOCK))
    scale_factor = head_dim ** (-0.5)
    query_blocks = queries.reshape(block_count, BLOCK, head_dim)
    key_blocks = keys_in.reshape(block_count, BLOCK, head_dim)
    value_blocks = values_in.reshape(block_count, BLOCK, head_dim)
    grad_blocks = grads_in.reshape(block_count, BLOCK, head_dim)
    seg_blocks = segments.reshape(block_count, BLOCK)
    owner_rows = lax.broadcasted_iota(jnp.int32, (block_count, group_size * select), 0)

    def one_group(carried, group_index):
        key_acc, value_acc = carried
        first_block = group_index * group_size
        chosen = lax.dynamic_slice_in_dim(blocks, first_block, group_size, 0).reshape(-1)
        query_part = lax.dynamic_slice_in_dim(query_blocks, first_block, group_size, 0)
        grad_part = lax.dynamic_slice_in_dim(grad_blocks, first_block, group_size, 0)
        query_segs = lax.dynamic_slice_in_dim(seg_blocks, first_block, group_size, 0)
        key_part = key_blocks[chosen].reshape(group_size, select * BLOCK, head_dim)
        value_part = value_blocks[chosen].reshape(group_size, select * BLOCK, head_dim)
        key_segs = seg_blocks[chosen].reshape(group_size, select * BLOCK)
        live_mask = query_segs[:, :, None] == key_segs[:, None, :]
        scores = (
            jnp.einsum("nqd,nkd->nqk", query_part, key_part, preferred_element_type=jnp.float32)
            * scale_factor
        )
        scores = jnp.where(live_mask, scores, -1e30)
        top_score = jnp.max(scores, axis=2, keepdims=True)
        weights = jnp.where(live_mask, jnp.exp(scores - top_score), 0.0)
        soft_probs = weights / jnp.sum(weights, axis=2, keepdims=True)
        probs_bf = soft_probs.astype(jnp.bfloat16)
        attended = jnp.einsum(
            "nqk,nkd->nqd", probs_bf, value_part, preferred_element_type=jnp.float32
        ).astype(jnp.bfloat16)
        row_delta = jnp.sum(
            grad_part.astype(jnp.float32) * attended.astype(jnp.float32), axis=2, keepdims=True
        )
        d_probs = jnp.einsum(
            "nqd,nkd->nqk", grad_part, value_part, preferred_element_type=jnp.float32
        )
        d_scores = (soft_probs * (d_probs - row_delta) * scale_factor).astype(jnp.bfloat16)
        d_query = jnp.einsum(
            "nqk,nkd->nqd", d_scores, key_part, preferred_element_type=jnp.float32
        ).astype(jnp.bfloat16)
        key_terms = jnp.einsum(
            "nqk,nqd->nkd", d_scores, query_part, preferred_element_type=jnp.float32
        ).reshape(group_size * select, BLOCK * head_dim)
        value_terms = jnp.einsum(
            "nqk,nqd->nkd", probs_bf, grad_part, preferred_element_type=jnp.float32
        ).reshape(group_size * select, BLOCK * head_dim)
        owner_map = (owner_rows == chosen[None, :]).astype(jnp.float32)
        key_acc = key_acc + jnp.dot(
            owner_map,
            key_terms,
            precision=lax.Precision.HIGHEST,
            preferred_element_type=jnp.float32,
        )
        value_acc = value_acc + jnp.dot(
            owner_map,
            value_terms,
            precision=lax.Precision.HIGHEST,
            preferred_element_type=jnp.float32,
        )
        return ((key_acc, value_acc), (attended, d_query))

    blank_acc = jnp.zeros((block_count, BLOCK * head_dim), jnp.float32)
    sums, stacked = lax.scan(
        one_group, (blank_acc, blank_acc), jnp.arange(block_count // group_size, dtype=jnp.int32)
    )
    return (
        stacked[0].reshape(seq_len, head_dim),
        stacked[1].reshape(seq_len, head_dim),
        sums[0].reshape(seq_len, head_dim).astype(jnp.bfloat16),
        sums[1].reshape(seq_len, head_dim).astype(jnp.bfloat16),
    )


def general_device(tokens, w_query, w_key, w_value, w_output, grad_out, doc_lengths, block_ids):
    tok_rows = tokens[0]
    cotangent = grad_out[0]
    tok_dev, width = tok_rows.shape
    ctx_size = lax.axis_size("ctx")
    local_heads = HEADS // ctx_size
    head_band = local_heads * HEAD_DIM
    group_rows = (
        lax.all_gather(w_query, "ctx", axis=0, tiled=True),
        lax.all_gather(w_key, "ctx", axis=0, tiled=True),
        lax.all_gather(w_value, "ctx", axis=0, tiled=True),
        lax.all_gather(w_output, "ctx", axis=0, tiled=True),
    )
    pieces = (
        lax.all_gather(group_rows[0], "fsdp", axis=0, tiled=True),
        lax.all_gather(group_rows[1], "fsdp", axis=0, tiled=True),
        lax.all_gather(group_rows[2], "fsdp", axis=0, tiled=True),
        lax.all_gather(group_rows[3], "fsdp", axis=0, tiled=True),
    )
    tok_part = tok_rows
    query_acc = jnp.dot(tok_part, pieces[0], preferred_element_type=jnp.float32)
    key_acc = jnp.dot(tok_part, pieces[1], preferred_element_type=jnp.float32)
    value_acc = jnp.dot(tok_part, pieces[2], preferred_element_type=jnp.float32)
    grad_acc = contract_last(cotangent, pieces[3])
    queries = query_acc.astype(jnp.bfloat16)
    keys_all = key_acc.astype(jnp.bfloat16)
    values_all = value_acc.astype(jnp.bfloat16)
    d_attended = grad_acc.astype(jnp.bfloat16)

    def to_band(matrix):
        return matrix.reshape(tok_dev, ctx_size, head_band)

    received = (
        lax.all_to_all(to_band(queries), "ctx", split_axis=1, concat_axis=0, tiled=True),
        lax.all_to_all(to_band(keys_all), "ctx", split_axis=1, concat_axis=0, tiled=True),
        lax.all_to_all(to_band(values_all), "ctx", split_axis=1, concat_axis=0, tiled=True),
        lax.all_to_all(to_band(d_attended), "ctx", split_axis=1, concat_axis=0, tiled=True),
    )
    query_heads = received[0].reshape(-1, head_band)
    key_heads = received[1].reshape(-1, head_band)
    value_heads = received[2].reshape(-1, head_band)
    grad_heads = received[3].reshape(-1, head_band)
    seq_len = query_heads.shape[0]
    segments = segment_ids(doc_lengths[0], seq_len)
    head_base = lax.axis_index("ctx") * local_heads

    def per_head(head_index, buffers):
        column = head_index * HEAD_DIM

        def columns(matrix):
            return lax.dynamic_slice_in_dim(matrix, column, HEAD_DIM, 1)

        blocks = lax.dynamic_slice_in_dim(block_ids, head_base + head_index, 1, 0)[0]
        results = head_pass(
            columns(query_heads),
            columns(key_heads),
            columns(value_heads),
            columns(grad_heads),
            blocks,
            segments,
        )
        return (
            lax.dynamic_update_slice_in_dim(buffers[0], results[0], column, 1),
            lax.dynamic_update_slice_in_dim(buffers[1], results[1], column, 1),
            lax.dynamic_update_slice_in_dim(buffers[2], results[2], column, 1),
            lax.dynamic_update_slice_in_dim(buffers[3], results[3], column, 1),
        )

    blank_band = jnp.zeros((seq_len, head_band), jnp.bfloat16)
    buffers = lax.fori_loop(
        0, local_heads, per_head, (blank_band, blank_band, blank_band, blank_band)
    )

    def to_rows(matrix):
        return matrix.reshape(seq_len, 1, head_band)

    returned = (
        lax.all_to_all(to_rows(buffers[0]), "ctx", split_axis=0, concat_axis=1, tiled=True),
        lax.all_to_all(to_rows(buffers[1]), "ctx", split_axis=0, concat_axis=1, tiled=True),
        lax.all_to_all(to_rows(buffers[2]), "ctx", split_axis=0, concat_axis=1, tiled=True),
        lax.all_to_all(to_rows(buffers[3]), "ctx", split_axis=0, concat_axis=1, tiled=True),
    )
    attended = returned[0].reshape(tok_dev, width)
    d_query = returned[1].reshape(tok_dev, width)
    d_key = returned[2].reshape(tok_dev, width)
    d_value = returned[3].reshape(tok_dev, width)
    pieces = (
        lax.all_gather(group_rows[0], "fsdp", axis=0, tiled=True),
        lax.all_gather(group_rows[1], "fsdp", axis=0, tiled=True),
        lax.all_gather(group_rows[2], "fsdp", axis=0, tiled=True),
        lax.all_gather(group_rows[3], "fsdp", axis=0, tiled=True),
    )
    out_acc = tok_rows.astype(jnp.float32)
    att_part = attended
    out_acc = out_acc + jnp.dot(att_part, pieces[3], preferred_element_type=jnp.float32)
    update = (
        contract_last(d_query, pieces[0])
        + contract_last(d_key, pieces[1])
        + contract_last(d_value, pieces[2])
    )
    grad_acc = update
    layer_out = out_acc.astype(jnp.bfloat16)
    grad_tokens = (cotangent.astype(jnp.float32) + grad_acc).astype(jnp.bfloat16)
    total_tokens = tok_dev * lax.axis_size("dp") * lax.axis_size("fsdp") * ctx_size
    grad_scale = total_tokens ** (-0.5)
    tok_part = tok_rows
    att_part = attended
    summed = lax.psum_scatter(
        jnp.concatenate(
            [
                contract_first(tok_part, d_query),
                contract_first(tok_part, d_key),
                contract_first(tok_part, d_value),
                contract_first(att_part, cotangent),
            ],
            axis=1,
        )
        * grad_scale,
        ("fsdp", "ctx"),
        scatter_dimension=0,
        tiled=True,
    )
    summed = lax.psum(summed, "dp")
    return (
        layer_out[None],
        grad_tokens[None],
        summed[:, 0:width],
        summed[:, width : 2 * width],
        summed[:, 2 * width : 3 * width],
        summed[:, 3 * width : 4 * width],
    )


def attention_kernel(
    logs_ref, seg_row_ref, seg_col_ref, q_ref, k_ref, v_ref, g_ref,
    att_ref, dq_ref, dk_ref, dv_ref, dk_acc, dv_acc,
):
    seq_len, lanes = q_ref.shape
    heads_here = lanes // HEAD_DIM
    block_count = seq_len // BLOCK
    tile = BLOCK * (2 if block_count % 2 == 0 else 1)
    scale_factor = HEAD_DIM ** (-0.5)
    lane_ids = lax.broadcasted_iota(jnp.int32, (1, lanes), 1) // HEAD_DIM
    keys = k_ref[...]
    values = v_ref[...]
    dk_acc[...] = jnp.zeros_like(dk_acc)
    dv_acc[...] = jnp.zeros_like(dv_acc)
    seg_keys = seg_col_ref[...]
    zero = jnp.zeros((), jnp.bfloat16)

    for part in range(seq_len // tile):
        rows = pl.ds(part * tile, tile)
        query_part = q_ref[rows, :] * jnp.asarray(scale_factor, jnp.bfloat16)
        grad_part = g_ref[rows, :]
        live = seg_keys == seg_row_ref[:, rows]
        att_sum = jnp.zeros((tile, lanes), jnp.float32)
        dq_sum = jnp.zeros((tile, lanes), jnp.float32)
        for head in range(heads_here):
            mine = lane_ids == head
            q_head = jnp.where(mine, query_part, zero)
            g_head = jnp.where(mine, grad_part, zero)
            scores = contract_last(keys, q_head)
            bias = jnp.broadcast_to(
                logs_ref[head, :, rows][:, None, :], (block_count, BLOCK, tile)
            ).reshape(seq_len, tile)
            scores = jnp.where(live, scores + bias, -1e30)
            top_score = jnp.max(scores, axis=0, keepdims=True)
            weights = jnp.exp(scores - top_score)
            inverse = 1.0 / jnp.sum(weights, axis=0, keepdims=True)
            probs = weights * inverse
            d_probs = contract_last(values, g_head)
            row_delta = jnp.sum(probs * d_probs, axis=0, keepdims=True)
            probs_bf = probs.astype(jnp.bfloat16)
            d_scores = (probs * (d_probs - row_delta)).astype(jnp.bfloat16)
            att_sum = jnp.where(mine, contract_first(probs_bf, values), att_sum)
            dq_sum = jnp.where(mine, contract_first(d_scores, keys), dq_sum)
            dv_acc[...] += jnp.dot(probs_bf, g_head, preferred_element_type=jnp.float32)
            dk_acc[...] += jnp.dot(d_scores, q_head, preferred_element_type=jnp.float32)
        att_ref[rows, :] = att_sum.astype(jnp.bfloat16)
        dq_ref[rows, :] = (dq_sum * scale_factor).astype(jnp.bfloat16)
    dk_ref[...] = dk_acc[...].astype(jnp.bfloat16)
    dv_ref[...] = dv_acc[...].astype(jnp.bfloat16)


def attention(queries, keys, values, grads, logs, segments, stripe):
    seq_len, band = queries.shape
    heads_here = stripe // HEAD_DIM
    block_count = logs.shape[1]
    whole = pl.BlockSpec((seq_len, stripe), lambda i: (0, i))
    return pl.pallas_call(
        attention_kernel,
        grid=(band // stripe,),
        out_shape=[jax.ShapeDtypeStruct((seq_len, band), jnp.bfloat16)] * 4,
        in_specs=[
            pl.BlockSpec((heads_here, block_count, seq_len), lambda i: (i, 0, 0)),
            pl.BlockSpec((1, seq_len), lambda i: (0, 0)),
            pl.BlockSpec((seq_len, 1), lambda i: (0, 0)),
            whole, whole, whole, whole,
        ],
        out_specs=[whole] * 4,
        scratch_shapes=[pltpu.VMEM((seq_len, stripe), jnp.float32)] * 2,
        compiler_params=pltpu.CompilerParams(vmem_limit_bytes=48 * 1024 * 1024),
        name="attention",
    )(logs, segments[None, :], segments[:, None], queries, keys, values, grads)


def block_logs(blocks, seq_len):
    block_count = blocks.shape[1]
    ids = jnp.arange(block_count, dtype=jnp.int32)
    counts = jnp.sum((blocks[:, None, :, :] == ids[None, :, None, None]).astype(jnp.float32), 3)
    logs = jnp.where(counts > 0, jnp.log(jnp.maximum(counts, 1.0)), -1e30)
    return jnp.repeat(logs, seq_len // block_count, axis=2)


def striped_device(tokens, w_query, w_key, w_value, w_output, grad_out, doc_lengths, block_ids):
    tok_rows = tokens[0]
    cotangent = grad_out[0]
    tok_dev, width = tok_rows.shape
    rows = w_query.shape[0]
    dp_size, fsdp_size = lax.axis_size("dp"), lax.axis_size("fsdp")
    ctx_size = 2
    me = lax.axis_index("ctx")
    swap = [(0, 1), (1, 0)]
    band = fsdp_size * rows
    seq_len = tok_dev * ctx_size
    share = rows // dp_size

    def other(matrix):
        return lax.ppermute(matrix, "ctx", swap)

    dp_bits, fsdp_bits = dp_size.bit_length() - 1, fsdp_size.bit_length() - 1

    def flip(matrix, axis, size, bit):
        return lax.ppermute(matrix, axis, [(i, i ^ (1 << bit)) for i in range(size)])

    def join(block, axis, size, bit):
        peer = flip(block, axis, size, bit)
        low = (lax.axis_index(axis) >> bit) % 2 == 0
        return jnp.stack([jnp.where(low, block, peer), jnp.where(low, peer, block)])

    def fold(block, axis, size, bit):
        side = (lax.axis_index(axis) >> bit) % 2
        given = flip(lax.dynamic_index_in_dim(block, 1 - side, 0, False), axis, size, bit)
        kept = lax.dynamic_index_in_dim(block, side, 0, False)
        return (kept.astype(jnp.float32) + given.astype(jnp.float32)).astype(jnp.bfloat16)

    def ordered(own, peer):
        first = me == 0
        return jnp.stack([jnp.where(first, own, peer), jnp.where(first, peer, own)])

    tok_peer = other(tok_rows)
    cot_peer = other(cotangent)

    start = lax.axis_index("dp") * share

    def my_share(matrix):
        return lax.dynamic_slice_in_dim(matrix, start, share, 0)

    qkv = jnp.stack([my_share(w_query), my_share(w_key), my_share(w_value)], axis=1)
    qkv = qkv.reshape(share, 3, fsdp_size, ctx_size, rows)
    kept = lax.dynamic_index_in_dim(qkv, me, 3, False).reshape(share, 3 * band)
    sent = lax.dynamic_index_in_dim(qkv, 1 - me, 3, False).reshape(share, 3 * band)
    qkv = ordered(kept, other(sent))
    out_share = my_share(w_output).reshape(share, ctx_size, width // 2).transpose(1, 0, 2)

    def spread(block):
        for bit in reversed(range(fsdp_bits)):
            block = join(block, "fsdp", fsdp_size, bit)
        for bit in reversed(range(dp_bits)):
            block = join(block, "dp", dp_size, bit)
        block = block.reshape((2,) * (dp_bits + fsdp_bits) + block.shape[-3:])
        dp_dims = tuple(reversed(range(dp_bits)))
        fsdp_dims = tuple(dp_bits + d for d in reversed(range(fsdp_bits)))
        last = dp_bits + fsdp_bits
        return block, fsdp_dims, dp_dims, last

    qk_block, fsdp_dims, dp_dims, last = spread(qkv[..., : 2 * band])
    vo_block = spread(jnp.concatenate([qkv[..., 2 * band :], out_share], axis=2))[0]
    row_order = fsdp_dims + (last,) + dp_dims + (last + 1, last + 2)
    out_order = fsdp_dims + dp_dims + (last + 1, last, last + 2)
    w_qk = qk_block.transpose(row_order).reshape(width, 2 * band)
    w_value_all = vo_block[..., :band].transpose(row_order).reshape(width, band)
    w_out = vo_block[..., band:].transpose(out_order).reshape(band, width)

    tok_all = ordered(tok_rows, tok_peer).reshape(seq_len, width)
    cot_all = ordered(cotangent, cot_peer).reshape(seq_len, width)
    queries = jnp.dot(
        tok_all, w_qk[:, :band], preferred_element_type=jnp.float32
    ).astype(jnp.bfloat16)
    keys = jnp.dot(
        tok_all, w_qk[:, band:], preferred_element_type=jnp.float32
    ).astype(jnp.bfloat16)
    values = jnp.dot(
        tok_all, w_value_all, preferred_element_type=jnp.float32
    ).astype(jnp.bfloat16)
    d_attended = contract_last(cot_all, w_out).astype(jnp.bfloat16)

    segments = segment_ids(doc_lengths[0], seq_len)
    stripe_heads = rows // HEAD_DIM
    my_blocks = lax.dynamic_index_in_dim(
        block_ids.reshape((fsdp_size, ctx_size, stripe_heads) + block_ids.shape[1:]), me, 1, False
    ).reshape((fsdp_size * stripe_heads,) + block_ids.shape[1:])
    logs = block_logs(my_blocks, seq_len)
    attended, d_query, d_key, d_value = attention(
        queries, keys, values, d_attended, logs, segments, rows
    )
    d_qk = jnp.concatenate([d_query, d_key], axis=1)

    total_tokens = tok_dev * dp_size * fsdp_size * ctx_size
    grad_scale = total_tokens ** (-0.5)
    halves = (2,) * fsdp_bits, (2,) * dp_bits

    def scaled(product):
        return (product * grad_scale).astype(jnp.bfloat16)

    def row_parts(matrix):
        columns = matrix.shape[1]
        parts = matrix.reshape(halves[0] + (ctx_size,) + halves[1] + (share, columns))
        dp_dims = tuple(fsdp_bits + 1 + d for d in reversed(range(dp_bits)))
        fsdp_dims = tuple(reversed(range(fsdp_bits)))
        rest = dp_bits + fsdp_bits + 1
        return parts.transpose(dp_dims + fsdp_dims + (fsdp_bits, rest, rest + 1))

    g_out = scaled(contract_first(attended, cot_all))
    out_parts = g_out.reshape(halves[0] + halves[1] + (share, ctx_size, width // 2))
    rest = dp_bits + fsdp_bits
    out_parts = out_parts.transpose(
        tuple(reversed(range(rest)))[:dp_bits]
        + tuple(reversed(range(fsdp_bits)))
        + (rest + 1, rest, rest + 2)
    )
    vo_sum = jnp.concatenate(
        [row_parts(scaled(contract_first(tok_all, d_value))), out_parts], axis=-1
    )
    qk_sum = row_parts(scaled(contract_first(tok_all, d_qk)))
    for bit in range(dp_bits):
        vo_sum = fold(vo_sum, "dp", dp_size, bit)
        qk_sum = fold(qk_sum, "dp", dp_size, bit)
    out_part = jnp.dot(attended, w_out, preferred_element_type=jnp.float32)
    tok_part = contract_last(d_qk, w_qk) + contract_last(d_value, w_value_all)
    out_part = out_part.reshape(ctx_size, tok_dev, width)
    tok_part = tok_part.reshape(ctx_size, tok_dev, width)

    def pick(matrix, index):
        return lax.dynamic_index_in_dim(matrix, index, 0, False)

    out_give = pick(out_part, 1 - me).astype(jnp.bfloat16)
    tok_give = pick(tok_part, 1 - me).astype(jnp.bfloat16)
    out_sent = other(out_give)
    tok_sent = other(tok_give)
    qk_sum, out_sent = lax.optimization_barrier((qk_sum, out_sent))
    for bit in range(fsdp_bits):
        vo_sum = fold(vo_sum, "fsdp", fsdp_size, bit)
        qk_sum = fold(qk_sum, "fsdp", fsdp_size, bit)
        if bit == 0:
            qk_sum, tok_sent = lax.optimization_barrier((qk_sum, tok_sent))

    def over_ctx(matrix):
        kept = lax.dynamic_index_in_dim(matrix, me, 0, False)
        sent = lax.dynamic_index_in_dim(matrix, 1 - me, 0, False)
        return ordered(kept, other(sent))

    def over_dp(block):
        for bit in reversed(range(dp_bits)):
            block = join(block, "dp", dp_size, bit)
        dims = tuple(reversed(range(dp_bits))) + tuple(range(dp_bits, block.ndim))
        return block.transpose(dims).reshape((dp_size,) + block.shape[dp_bits:])

    vo_final = over_dp(
        jnp.concatenate([over_ctx(vo_sum[..., :band]), vo_sum[..., band:]], axis=2)
    )
    qk_final = over_dp(over_ctx(qk_sum))

    def full_rows(block):
        block = block.reshape(dp_size, ctx_size, share, fsdp_size, rows)
        return block.transpose(0, 2, 3, 1, 4).reshape(rows, width).astype(jnp.float32)

    f_out = vo_final[..., band:].transpose(0, 2, 1, 3).reshape(rows, width).astype(jnp.float32)

    layer_out = tok_rows.astype(jnp.float32) + pick(out_part, me) + out_sent.astype(jnp.float32)
    grad_tokens = cotangent.astype(jnp.float32) + pick(tok_part, me) + tok_sent.astype(jnp.float32)
    return (
        layer_out.astype(jnp.bfloat16)[None],
        grad_tokens.astype(jnp.bfloat16)[None],
        full_rows(qk_final[..., :band]),
        full_rows(qk_final[..., band:]),
        full_rows(vo_final[..., :band]),
        f_out,
    )


def per_device(tokens, w_query, w_key, w_value, w_output, grad_out, doc_lengths, block_ids):
    rows = w_query.shape[0]
    dp_size, fsdp_size = lax.axis_size("dp"), lax.axis_size("fsdp")
    striped = (
        lax.axis_size("ctx") == 2
        and dp_size & (dp_size - 1) == 0
        and fsdp_size & (fsdp_size - 1) == 0
        and rows % 128 == 0
        and rows % HEAD_DIM == 0
        and rows % (dp_size * 16) == 0
    )
    body = striped_device if striped else general_device
    return body(tokens, w_query, w_key, w_value, w_output, grad_out, doc_lengths, block_ids)


def solution(mesh):
    in_specs = (
        P(("dp", "fsdp"), "ctx", None),
        P(("fsdp", "ctx"), None),
        P(("fsdp", "ctx"), None),
        P(("fsdp", "ctx"), None),
        P(("fsdp", "ctx"), None),
        P(("dp", "fsdp"), "ctx", None),
        P(("dp", "fsdp"), None),
        P(),
    )
    out_specs = (
        P(("dp", "fsdp"), "ctx", None),
        P(("dp", "fsdp"), "ctx", None),
        P(("fsdp", "ctx"), None),
        P(("fsdp", "ctx"), None),
        P(("fsdp", "ctx"), None),
        P(("fsdp", "ctx"), None),
    )
    return jax.shard_map(
        per_device, mesh=mesh, in_specs=in_specs, out_specs=out_specs, check_vma=False
    )
```
